512 devices in a mesh: gx: 32 (over x_lo, z), gy: 16 (over x_hi, y, core).
Axes of the slice: x: 4 (x_hi: 2, x_lo: 2; x = x_hi * 2 + x_lo), y: 4, z: 16, core: 2. Of those that a mesh axis runs over, the one named last changes fastest.
Arguments:
- hidden_in: bfloat16 [2048, 16384], P('gy', 'gx'), may hold values from -200 to 200
- norm_gain: float32 [16384], P('gx'), may hold values from 0.1 to 1.9
- w_query: bfloat16 [16384, 8192], P('gx', 'gy'), may hold values from -24 to 24
- w_key: bfloat16 [16384, 1024], P('gx'), may hold values from -1 to 1
- w_value: bfloat16 [16384, 1024], P('gx'), may hold values from -0.046875 to 0.046875
- w_out: bfloat16 [8192, 16384], P('gy', 'gx'), may hold values from -0.06591797 to 0.06591797
- seg_lengths: int32 [8], replicated, may hold values from 1 to 512, 2048 in all
Outputs:
- update: bfloat16 [2048, 16384], P('gy', 'gx')
The draws below stay inside these ranges and needn't reach their ends.
Inputs may be any that keep to these rules, and one draw needn't show every extreme that they name: `seg_lengths`: the 8 lengths sum to 2048 and the longest is exactly 512.
All inputs are finite; a program needn't handle non-finite values.
Results may differ from the reference program's by a relative error of at most 0.04.
Values may be sent and summed in bfloat16 or wider, within the bound.
A program may use at most 64 MiB of HBM per device.

```python
import math
import jax
import jax.numpy as jnp
import numpy as np
from jax import lax

D = 16384
H = 64
KVH = 8
HD = 128
TOKENS = 2048
SEGS = 8
SEG_MOST = 512
N_GX = 32
N_GY = 16


def shared_keys(key):
    return jnp.clip(jax.random.normal(key, (D, KVH * HD), jnp.float32), -6.0, 6.0) * D ** (-0.5)


def draw_w_key(key, part):
    shared = shared_keys(key)
    return shared.astype(jnp.bfloat16)


def draw_w_query(key, part):
    key = jax.random.fold_in(key, 23)
    first_key = jax.random.fold_in(key, 0)
    base = jnp.clip(jax.random.normal(first_key, (D, H * HD), jnp.float32), -6.0, 6.0) * D ** (-0.5)
    return base.astype(jnp.bfloat16)


def draw_hidden_in(key, part):
    key = jax.random.fold_in(key, 5)
    col_key, row_key, noise_key = jax.random.split(key, 3)
    column = jnp.arange(D, dtype=jnp.float32) / D
    col_scale = jnp.exp(math.log(10.0) * 0.5 * (column + jax.random.uniform(col_key, (D,), jnp.float32)))
    row_scale = jnp.exp(math.log(10.0) * jax.random.uniform(row_key, (TOKENS, 1), jnp.float32))
    noise = jnp.clip(jax.random.normal(noise_key, (TOKENS, D), jnp.float32), -6.0, 6.0)
    return (0.3 * noise * col_scale[None, :] * row_scale).astype(jnp.bfloat16)


def spiked(array, rng, source, target, shards_of, factor):
    def block_of(dim):
        return (jnp.arange(array.shape[dim]) // (array.shape[dim] // shards_of)).reshape((-1,) + (1,) * (array.ndim - 1 - dim))

    one_side = jax.random.permutation(rng, shards_of)[block_of(target)]
    second = (block_of(target) + shards_of // 2) % shards_of
    return jnp.where((block_of(source) == one_side) | (block_of(source) == second), factor * array, array)


def block_scale(key, dims, pieces, least, high):
    factor_of, own = 1.0, jax.random.fold_in(key, 6)
    for dim, parts in pieces:
        heights = jnp.exp(jax.random.uniform(jax.random.fold_in(own, dim), (parts,), jnp.float32, least / len(pieces), high / len(pieces)))
        factor_of = factor_of * jnp.repeat(heights, dims[dim] // parts).reshape([-1 if axis == dim else 1 for axis in range(len(dims))])
    return factor_of


def split_up(number_of, total, limit, slope):
    loads = [(1 << 20) // math.isqrt(grade ** slope) + 1 for grade in range(2, number_of + 1)]
    surplus, given = total - limit - (number_of - 1), [1] * (number_of - 1)
    while surplus > 0:
        movable = [i for i in range(number_of - 1) if given[i] < limit]
        mass, budget = sum([loads[i] for i in movable]), surplus
        for i in movable:
            extra = min(limit - given[i], max(1, budget * loads[i] // mass), surplus)
            given[i] = given[i] + extra
            surplus = surplus - extra
    return np.array([limit] + given)


def ragged_sizes(rng, count, total, bound, slope):
    if count == 2:
        one = jax.random.randint(rng, (), max(1, total - bound), min(bound, total - 1) + 1)
        return jnp.stack([one, total - one])
    tallies = jnp.asarray(split_up(count, total, bound, slope), jnp.int32)
    twos = (count - 1) // 2
    giver, sink = tallies[1:1 + 2 * twos:2], tallies[2:2 + 2 * twos:2]
    room = jnp.minimum(giver - 1, bound - sink)
    moved = jax.random.randint(jax.random.fold_in(rng, 1), (twos,), 0, 1 << 20) % (room + 1)
    tallies = tallies.at[1:1 + 2 * twos:2].set(giver - moved).at[2:2 + 2 * twos:2].set(sink + moved)
    return tallies[jax.random.permutation(jax.random.fold_in(rng, 2), count)]


def gaussian(stream_key, shape, width, reach, shards=(), held_as=jnp.bfloat16):
    result = jax.random.normal(stream_key, shape, jnp.float32) * width
    if len(shards) > 0:
        result = block_scale(stream_key, shape, shards, -0.22, 0.18) * result
    return jnp.clip(result, min=-reach, max=reach).astype(held_as)


def noise_with(stream_key, shape, width, limit, cuts, heavy, kind=jnp.bfloat16):
    result = width * jax.random.normal(stream_key, shape, jnp.float32)
    if cuts:
        result = result * block_scale(stream_key, shape, cuts, -0.22, 0.18)
    return jnp.clip(spiked(result, jax.random.fold_in(stream_key, 3), *heavy), -limit, limit).astype(kind)


def setup_inputs(seed: int = 0) -> dict:
    splits = jax.random.split(jax.random.key(seed), 8)
    return {
        "hidden_in": draw_hidden_in(jax.random.fold_in(splits[7], 71), 0),
        "norm_gain": jnp.clip(1.0 + 0.18 * jax.random.normal(splits[1], (D,), jnp.float32), 0.1, 1.9),
        "w_query": draw_w_query(jax.random.fold_in(splits[7], 71), 0),
        "w_key": draw_w_key(jax.random.fold_in(splits[7], 71), 0),
        "w_value": gaussian(splits[4], (D, KVH * HD), D ** -0.5, 0.046875, ((0, 32),)),
        "w_out": noise_with(splits[5], (H * HD, D), ((H * HD) ** -0.5), 0.06591797, ((0, 16), (1, 32)), (0, 1, 32, 2.75)),
        "seg_lengths": ragged_sizes(splits[6], SEGS, TOKENS, SEG_MOST, 2).astype(jnp.int32),
    }


ROPE_BASE = 500000.0
EPS = 1e-05

def rotate(values, position, head_size):
    half = head_size // 2
    exponent = jnp.arange(half, dtype=jnp.float32) * (2.0 / head_size)
    frequency = ROPE_BASE ** (-exponent)
    angle = position[:, None, None] * frequency[None, None, :]
    cosine = jnp.cos(angle)
    sine = jnp.sin(angle)
    first = values[..., :half]
    second = values[..., half:]
    return jnp.concatenate([first * cosine - second * sine, second * cosine + first * sine], axis=-1)

def segment_table(seg_lengths, tokens):
    ends = jnp.cumsum(seg_lengths).astype(jnp.int32)
    starts = (ends - seg_lengths).astype(jnp.int32)
    index = jnp.arange(tokens, dtype=jnp.int32)
    member = ((index[:, None] >= starts[None, :]) & (index[:, None] < ends[None, :])).astype(jnp.int32)
    seg_id = lax.optimization_barrier(jnp.sum(member * jnp.arange(seg_lengths.shape[0], dtype=jnp.int32)[None, :], axis=1)).astype(jnp.int32)
    first_index = lax.optimization_barrier(jnp.sum(member * starts[None, :], axis=1)).astype(jnp.int32)
    return (seg_id, (index - first_index).astype(jnp.int32))

def block_sum(left, right, blocks):
    total_rows = left.shape[0]
    block_width = left.shape[1] // blocks
    left_blocks = left.reshape(total_rows, blocks, block_width).transpose(1, 0, 2)
    right_blocks = right.reshape(blocks, block_width, right.shape[1])

    def add_block(total, pair):
        product = jnp.dot(pair[0], pair[1], preferred_element_type=jnp.float32)
        rounded = lax.optimization_barrier(product.astype(jnp.bfloat16))
        return (total + rounded.astype(jnp.float32), None)
    start_total = jnp.zeros((total_rows, right.shape[1]), jnp.float32)
    total, _ = lax.scan(add_block, start_total, (left_blocks, right_blocks))
    return total

def reference(hidden_in, norm_gain, w_query, w_key, w_value, w_out, seg_lengths):
    widened = hidden_in.astype(jnp.float32)
    squares = lax.optimization_barrier(jnp.sum(widened * widened, axis=1))
    scale = lax.rsqrt(squares / D + EPS)
    normed = (widened * scale[:, None] * norm_gain.astype(jnp.float32)[None, :]).astype(jnp.bfloat16)
    query_sum = block_sum(normed, w_query, N_GX)
    key_raw = block_sum(normed, w_key, N_GX).astype(jnp.bfloat16)
    value_raw = block_sum(normed, w_value, N_GX).astype(jnp.bfloat16)
    seg_id, position = segment_table(seg_lengths, TOKENS)
    position_f = position.astype(jnp.float32)
    queries = rotate(query_sum.reshape(TOKENS, H, HD), position_f, HD).astype(jnp.bfloat16)
    keys = rotate(key_raw.astype(jnp.float32).reshape(TOKENS, KVH, HD), position_f, HD).astype(jnp.bfloat16)
    group = H // KVH
    query_groups = queries.reshape(TOKENS, KVH, group, HD).transpose(1, 2, 0, 3)
    key_groups = keys.transpose(1, 0, 2)
    value_groups = value_raw.reshape(TOKENS, KVH, HD).transpose(1, 0, 2)
    index = jnp.arange(TOKENS, dtype=jnp.int32)
    allowed = (seg_id[:, None] == seg_id[None, :]) & (index[None, :] <= index[:, None])

    def one_group(operands):
        query_part, key_part, value_part = operands
        scores = jnp.einsum('gtd,sd->gts', query_part.astype(jnp.float32), key_part.astype(jnp.float32)) * HD ** (-0.5)
        scores = jnp.where(allowed[None], scores, -jnp.inf)
        largest = lax.optimization_barrier(jnp.max(scores, axis=-1, keepdims=True))
        expo = jnp.exp(scores - largest)
        denominator = lax.optimization_barrier(jnp.sum(expo, axis=-1, keepdims=True))
        weights = expo.astype(jnp.bfloat16)
        summed = jnp.einsum('gts,sd->gtd', weights.astype(jnp.float32), value_part.astype(jnp.float32))
        return (summed / denominator).astype(jnp.bfloat16)
    attended = lax.map(one_group, (query_groups, key_groups, value_groups))
    attended = attended.transpose(2, 0, 1, 3).reshape(TOKENS, H * HD)
    return block_sum(attended, w_out, N_GY).astype(jnp.bfloat16)
```

```python
import math

import jax
import jax.numpy as jnp
from jax import lax
from jax.experimental import pallas as pl
from jax.experimental.pallas import tpu as pltpu
from jax.sharding import PartitionSpec as P

MESH = pl.DeviceIdType.MESH
HD = 128
HALF = HD // 2
SEGS = 8
ROPE_BASE = 500000.0
EPS = 1e-05
BF = jnp.bfloat16
F32 = jnp.float32

NZ = 16
TB = 128
TH = 64
WIDTH = 512
QF = 256
XF = HD + QF
ZF = WIDTH - QF
MSG = XF + 2 * ZF
RS = 32
WIN = 5
KEYS = WIN * TB
MODEL = 16384


def body(h, gain, wq, wk, wv, wo, seg, out, *s):
    (
        gath, wraw, kvraw, wcat, wov, gv, part, xs, xr, zs, zr, sq, sqs, sqr, sqx, fxs, fxr, kvw, af, al, cs, cr, own, es, er, el, ex,
        in_sem, ga_s, ga_r, x_s, x_r, z_s, z_r, q_s, q_r, f_s, f_r, kz_s, kx_s, kc_s, k_r,
        dz_s, dx_s, d_r, c_s, c_r, e_s, e_r, ex_s, ex_r,
    ) = s
    gx = lax.axis_index("gx")
    gy = lax.axis_index("gy")
    xlo, z = lax.div(gx, NZ), lax.rem(gx, NZ)
    xhi, y, core = lax.div(gy, 8), lax.rem(lax.div(gy, 2), 4), lax.rem(gy, 2)
    xot, hot, cot = 1 - xlo, 1 - xhi, 1 - core

    def zm(v):
        return lax.rem(v + NZ, NZ)

    def ym(v):
        return lax.rem(v + 4, 4)

    def at_z(d):
        return {"gx": xlo * NZ + zm(z + d), "gy": gy}

    def at_y(yy):
        return {"gx": gx, "gy": xhi * 8 + yy * 2 + core}

    dev_x = {"gx": xot * NZ + z, "gy": gy}
    dev_h = {"gx": gx, "gy": hot * 8 + y * 2 + core}
    dev_c = {"gx": gx, "gy": xhi * 8 + y * 2 + cot}

    def rc(src, dst, ss, rs, dev):
        return pltpu.make_async_remote_copy(src_ref=src, dst_ref=dst, send_sem=ss, recv_sem=rs, device_id=dev, device_id_type=MESH)

    barrier = pltpu.get_barrier_semaphore()
    greet = [dev_x, dev_h, dev_c] + [at_y(ym(y + d)) for d in (1, 2, 3)] + [at_z(d) for d in (1, 2, 3, 4, -1, -2, -3, -4)]
    for d in greet:
        pl.semaphore_signal(barrier, inc=1, device_id=d, device_id_type=MESH)
    head = pl.multiple_of((xhi * 4 + y) * HD, HD)
    cp_h = pltpu.make_async_copy(h, gath.at[gy], in_sem.at[0])
    cp_q = pltpu.make_async_copy(wq, wraw, in_sem.at[1])
    cp_o = pltpu.make_async_copy(wo, wov, in_sem.at[2])
    cp_g = pltpu.make_async_copy(gain, gv, in_sem.at[3])
    cp_k = pltpu.make_async_copy(wk.at[:, pl.ds(head, HD)], kvraw.at[0], in_sem.at[4])
    cp_v = pltpu.make_async_copy(wv.at[:, pl.ds(head, HD)], kvraw.at[1], in_sem.at[5])
    loads = [cp_h, cp_q, cp_o, cp_g, cp_k, cp_v]
    for c in loads:
        c.start()
    pl.semaphore_wait(barrier, len(greet))

    def gather_copy(blk, dev, n, src=None):
        return rc(gath.at[blk] if src is None else src, gath.at[blk], ga_s.at[n], ga_r.at[blk], dev)

    sends = []

    def go(c):
        c.start()
        sends.append(c)

    def blk(hh, yy, cc):
        return hh * 8 + yy * 2 + cc

    go(gather_copy(gy, dev_h, 0, h))
    for n, d in enumerate((1, 3, 2)):
        go(gather_copy(gy, at_y(ym(y + d)), 1 + n, h))
    go(gather_copy(gy, dev_c, 4, h))

    for c in loads:
        c.wait()
    gcol = jnp.transpose(jnp.broadcast_to(gv[...], (HD, WIDTH)))
    is_core0 = core == 0
    kv_w = jnp.where(is_core0, kvraw[0].astype(F32), kvraw[1].astype(F32))
    wcat[:, 0:HD] = (kv_w * gcol).astype(BF)
    for j in range(WIDTH // HD):
        wcat[:, HD * (j + 1) : HD * (j + 2)] = (wraw[:, HD * j : HD * (j + 1)].astype(F32) * gcol).astype(BF)

    far = blk(hot, y, core)
    gather_copy(far, dev_h, 0).wait_recv()
    for n, d in enumerate((1, 3, 2)):
        go(gather_copy(far, at_y(ym(y + d)), 5 + n))
    go(gather_copy(far, dev_c, 8))
    for n, d in enumerate((1, 3, 2)):
        for m, hh in enumerate((xhi, hot)):
            b = blk(hh, ym(y + d), core)
            gather_copy(b, dev_c, 9 + 2 * n + m).wait_recv()
            go(gather_copy(b, dev_c, 9 + 2 * n + m))
    for hh in (xhi, hot):
        for d in range(4):
            gather_copy(blk(hh, ym(y + d), cot), dev_c, 0).wait_recv()

    ones = jnp.ones((8, WIDTH), BF)
    nt = (((1,), (1,)), ((), ()))
    mine_top = xlo == 0

    def x_copy(b):
        return rc(xs.at[b], xr.at[b], x_s.at[b], x_r.at[b], dev_x)

    def z_copy(d, k, r):
        rows = pl.ds(r * RS, RS)
        return rc(zs.at[d, k, rows], zr.at[d, k, rows], z_s.at[d, k, r], z_r.at[d, k, r], at_z(1 - 2 * d))

    def q_copy(d, k):
        return rc(sqs.at[d, k], sqr.at[d, k], q_s.at[d, k], q_r.at[d, k], at_z(1 - 2 * d))

    def product(b):
        x = gath[b]
        res = jnp.dot(x, wcat[...], preferred_element_type=F32).astype(BF)
        top, bot = res[0:TH], res[TH:TB]
        part[b, :, 0:XF] = jnp.where(mine_top, top[:, 0:XF], bot[:, 0:XF])
        xs[b] = jnp.where(mine_top, bot[:, 0:XF], top[:, 0:XF])
        x_copy(b).start()
        part[b, :, XF : XF + ZF] = top[:, XF:]
        part[b, :, XF + ZF : MSG] = bot[:, XF:]
        xf = x.astype(F32)
        x2 = xf * xf
        hi = x2.astype(BF)
        lo = (x2 - hi.astype(F32)).astype(BF)
        sq[b] = lax.dot_general(ones, hi, nt, preferred_element_type=F32) + lax.dot_general(ones, lo, nt, preferred_element_type=F32)

    def own_rows(b, r):
        rows = slice(r * RS, r * RS + RS)
        a = part[b, rows, 0:XF].astype(F32) + xr[b, rows, :].astype(F32)
        return jnp.concatenate([a, part[b, rows, XF:MSG].astype(F32)], axis=1)

    def ring_step(d, k, b):
        x_copy(b).wait_recv()
        for r in range(2):
            rows = slice(r * RS, r * RS + RS)

            @pl.when(k == 0)
            def _():
                zs[d, k, rows, :] = own_rows(b, r).astype(BF)

            @pl.when(k > 0)
            def _():
                z_copy(d, k - 1, r).wait_recv()
                zs[d, k, rows, :] = (own_rows(b, r) + zr[d, k - 1, rows, :].astype(F32)).astype(BF)

            z_copy(d, k, r).start()

        @pl.when(k == 0)
        def _():
            sqs[d, k] = sq[b]

        @pl.when(k > 0)
        def _():
            q_copy(d, k - 1).wait_recv()
            sqs[d, k] = sq[b] + sqr[d, k - 1]

        q_copy(d, k).start()

    def reduce_step(i, _):
        @pl.when(i < 8)
        def _():
            product(zm(z + 8 - i))
            product(zm(z - 7 + i))

        @pl.when(i > 0)
        def _():
            ring_step(0, i - 1, zm(z + 9 - i))

        @pl.when((i > 0) & (i < 8))
        def _():
            ring_step(1, i - 1, zm(z - 8 + i))

        return 0

    lax.fori_loop(0, 9, reduce_step, 0)

    def firsts(tq):
        start = jnp.zeros_like(tq)
        total = jnp.int32(0)
        for i in range(SEGS):
            start = jnp.where(tq >= total, total, start)
            total = total + seg[i]
        return start

    here = z * TB + xlo * TH
    lane = lax.broadcasted_iota(jnp.int32, (TH, HD), 1)
    tok = here + lax.broadcasted_iota(jnp.int32, (TH, HD), 0)
    pos = (tok - firsts(tok)).astype(F32)
    freq = jnp.exp((lax.rem(lane, HALF)).astype(F32) * (-2.0 / HD * math.log(ROPE_BASE)))
    angle = pos * freq
    cosine = jnp.cos(angle)
    sine = jnp.sin(angle)
    sine = jnp.where(lane < HALF, -sine, sine)

    def rotated(v):
        return v * cosine + pltpu.roll(v, HALF, 1) * sine

    x_copy(z).wait_recv()
    fx = []
    totals = []
    for r in range(2):
        rows = slice(r * RS, r * RS + RS)
        z_copy(0, 7, r).wait_recv()
        z_copy(1, 6, r).wait_recv()
        t = own_rows(z, r) + zr[0, 7, rows, :].astype(F32) + zr[1, 6, rows, :].astype(F32)
        totals.append(t[:, 0:XF])
        fx.append(jnp.where(mine_top, t[:, XF : XF + ZF], t[:, XF + ZF : MSG]))
        fxs[rows, :] = jnp.where(mine_top, t[:, XF + ZF : MSG], t[:, XF : XF + ZF]).astype(BF)
    q_copy(0, 7).wait_recv()
    q_copy(1, 6).wait_recv()
    sqx[0] = sq[z] + sqr[0, 7] + sqr[1, 6]
    cp_sq = rc(sqx.at[0], sqx.at[1], f_s.at[0], f_r.at[0], dev_x)
    cp_fx = rc(fxs, fxr, f_s.at[1], f_r.at[1], dev_x)
    go(cp_sq)
    go(cp_fx)
    xsum = jnp.concatenate(totals, axis=0)
    zsum = jnp.concatenate(fx, axis=0)
    cp_sq.wait_recv()
    squares = jnp.transpose(jnp.broadcast_to((sqx[0] + sqx[1])[0:1], (HD, TB)))
    squares = jnp.where(mine_top, squares[0:TH], squares[TH:TB])
    scale = lax.rsqrt(squares / MODEL + EPS)

    def k_slot(d, xx, cc):
        return kvw.at[cc, d, xx]

    def k_copy(d, xx, cc, ss, dev, dd=None):
        return rc(k_slot(d, xx, cc), k_slot(d if dd is None else dd, xx, cc), ss, k_r.at[d if dd is None else dd, xx, cc], dev)

    kv = xsum[:, 0:HD] * scale
    kvw[core, 0, xlo] = jnp.where(is_core0, rotated(kv), kv).astype(BF)
    for d in range(1, WIN):
        go(k_copy(0, xlo, core, kz_s.at[d - 1], at_z(d), d))
    go(k_copy(0, xlo, core, kx_s.at[0], dev_x))
    go(k_copy(0, xlo, core, kc_s.at[0, xlo], dev_c))

    cp_fx.wait_recv()
    zsum = zsum + fxr[...].astype(F32)
    queries = [xsum[:, HD * (1 + j) : HD * (2 + j)] for j in range(2)] + [zsum[:, HD * j : HD * (j + 1)] for j in range(2)]
    queries = jnp.concatenate([rotated(q * scale).astype(BF) for q in queries], axis=0)

    for d in range(WIN):
        if d:
            k_copy(d, xlo, core, kx_s.at[d], dev_x).wait_recv()
            go(k_copy(d, xlo, core, kx_s.at[d], dev_x))
            go(k_copy(d, xlo, core, kc_s.at[d, xlo], dev_c))
        k_copy(d, xot, core, kx_s.at[d], dev_x).wait_recv()
        go(k_copy(d, xot, core, kc_s.at[d, xot], dev_c))
    for d in range(WIN):
        for xx in range(2):
            k_copy(d, xx, cot, kx_s.at[d], dev_c).wait_recv()

    keys = kvw[0].reshape(KEYS, HD)
    values = kvw[1].reshape(KEYS, HD)
    scores = lax.dot_general(queries, keys, nt, preferred_element_type=F32) * (1.0 / math.sqrt(HD))
    n = lax.broadcasted_iota(jnp.int32, (TH, KEYS), 1)
    tk = z * TB + n - 2 * TB * lax.div(n, TB)
    tq = here + lax.broadcasted_iota(jnp.int32, (TH, KEYS), 0)
    allowed = (tk >= firsts(tq)) & (tk <= tq)
    for j in range(4):
        sc = jnp.where(allowed, scores[TH * j : TH * (j + 1)], -1e30)
        e = jnp.exp(sc - jnp.max(sc, axis=1, keepdims=True))
        e = jnp.where(allowed, e, 0.0)
        o = jnp.dot(e.astype(BF), values, preferred_element_type=F32) / jnp.sum(e, axis=1, keepdims=True)
        ref = af if j < 2 else al
        ref[z, xlo, :, HD * (j % 2) : HD * (j % 2 + 1)] = o.astype(BF)

    def unit(u, b):
        return af.at[b, u] if u < 2 else al.at[b, xlo]

    def d_copy(d, u, k, b):
        return rc(unit(u, b), unit(u, b), dz_s.at[d, u, k], d_r.at[u, b], at_z(1 - 2 * d))

    def l_copy(b, xx):
        return rc(al.at[b, xx], al.at[b, xx], dx_s.at[b], d_r.at[3, b], dev_x)

    cp_f = rc(af.at[z, xlo], af.at[z, xlo], dx_s.at[NZ], d_r.at[xlo, z], dev_x)
    cp_f.start()
    l_copy(z, xlo).start()
    for d in range(2):
        rc(af.at[z, xlo], af.at[z, xlo], dz_s.at[d, xlo, 0], d_r.at[xlo, z], at_z(1 - 2 * d)).start()
        d_copy(d, 2, 0, z).start()
    rc(af.at[z, xot], af.at[z, xot], dx_s.at[NZ], d_r.at[xot, z], dev_x).wait_recv()
    for d in range(2):
        rc(af.at[z, xot], af.at[z, xot], dz_s.at[d, xot, 0], d_r.at[xot, z], at_z(1 - 2 * d)).start()

    def pass_on(d, k, b, last):
        for u in range(3):
            d_copy(d, u, k, b).wait_recv()

            @pl.when(k < last)
            def _():
                d_copy(d, u, k, b).start()

        l_copy(b, xlo).start()

    def c_copy(b):
        m = lax.div(b, 2)
        return rc(cs.at[m], cr.at[m], c_s.at[m], c_r.at[m], dev_c)

    def e_copy(b, yy, src_y):
        hh = lax.div(b, 8)
        return rc(es.at[lax.div(b, 2)], er.at[hh, src_y], e_s.at[lax.div(b, 2)], e_r.at[hh, src_y], at_y(yy))

    def out_product(b):
        l_copy(b, xot).wait_recv()
        p = jnp.dot(af[b].reshape(TB, QF), wov[0:QF], preferred_element_type=F32)
        p = p + jnp.dot(al[b].reshape(TB, ZF), wov[QF:], preferred_element_type=F32)

        @pl.when(lax.rem(b, 2) == core)
        def _():
            own[lax.div(b, 2)] = p

        @pl.when(lax.rem(b, 2) != core)
        def _():
            cs[lax.div(b, 2)] = p.astype(BF)
            c_copy(b).start()

    def out_send(b):
        @pl.when(lax.rem(b, 2) == core)
        def _():
            c_copy(b).wait_recv()
            t = own[lax.div(b, 2)] + cr[lax.div(b, 2)].astype(F32)
            yb = lax.rem(lax.div(b, 2), 4)

            @pl.when(yb == y)
            def _():
                el[lax.div(b, 8)] = t

            @pl.when(yb != y)
            def _():
                es[lax.div(b, 2)] = t.astype(BF)
                e_copy(b, yb, y).start()

    def gather_step(k, _):
        pass_on(0, k, zm(z - k), 8)

        @pl.when(k < 8)
        def _():
            pass_on(1, k, zm(z + k), 7)

        out_product(zm(z - k + 1))

        @pl.when(k > 1)
        def _():
            out_product(zm(z + k - 1))
            out_send(zm(z - k + 2))

        @pl.when(k > 2)
        def _():
            out_send(zm(z + k - 2))

        return 0

    lax.fori_loop(1, 9, gather_step, 0)
    out_product(zm(z - 8))
    out_send(zm(z - 7))
    out_send(zm(z + 7))
    out_send(zm(z - 8))

    def y_sum(hh):
        t = el[hh]
        for d in range(1, 4):
            yy = ym(y + d)
            rc(es.at[0], er.at[hh, yy], e_s.at[0], e_r.at[hh, yy], at_y(yy)).wait_recv()
            t = t + er[hh, yy].astype(F32)
        return t

    ex[0] = y_sum(hot).astype(BF)
    cp_e = rc(ex.at[0], ex.at[1], ex_s, ex_r, dev_h)
    cp_e.start()
    mine = y_sum(xhi)
    cp_e.wait_recv()
    out[...] = (mine + ex[1].astype(F32)).astype(BF)

    for c in sends:
        c.wait_send()
    cp_e.wait_send()
    cp_f.wait_send()

    def left(b, _):
        x_copy(b).wait_send()
        l_copy(b, xlo).wait_send()
        return 0

    lax.fori_loop(0, NZ, left, 0)

    def left_z(k, _):
        for d in range(2):

            @pl.when(k < 8 - d)
            def _():
                for r in range(2):
                    z_copy(d, k, r).wait_send()
                q_copy(d, k).wait_send()
                for u in range(3):
                    d_copy(d, u, k, z).wait_send()

        b = 2 * k + cot
        c_copy(b).wait_send()

        @pl.when(lax.rem(k, 4) != y)
        def _():
            e_copy(2 * k, lax.rem(k, 4), y).wait_send()

        return 0

    lax.fori_loop(0, 8, left_z, 0)


def shards(hidden_in, norm_gain, w_query, w_key, w_value, w_out, seg_lengths):
    v = pltpu.VMEM
    dma = pltpu.SemaphoreType.DMA
    scratch = [
        v((NZ, TB, WIDTH), BF),
        v((WIDTH, WIDTH), BF),
        v((2, WIDTH, HD), BF),
        v((WIDTH, WIDTH + HD), BF),
        v((WIDTH, WIDTH), BF),
        v((1, WIDTH), F32),
        v((NZ, TH, MSG), BF),
        v((NZ, TH, XF), BF),
        v((NZ, TH, XF), BF),
        v((2, 8, TH, MSG), BF),
        v((2, 8, TH, MSG), BF),
        v((NZ, 8, TB), F32),
        v((2, 8, 8, TB), F32),
        v((2, 8, 8, TB), F32),
        v((2, 8, TB), F32),
        v((TH, ZF), BF),
        v((TH, ZF), BF),
        v((2, WIN, 2, TH, HD), BF),
        v((NZ, 2, TH, QF), BF),
        v((NZ, 2, TH, ZF), BF),
        v((8, TB, WIDTH), BF),
        v((8, TB, WIDTH), BF),
        v((8, TB, WIDTH), F32),
        v((8, TB, WIDTH), BF),
        v((2, 4, TB, WIDTH), BF),
        v((2, TB, WIDTH), F32),
        v((2, TB, WIDTH), BF),
        dma((6,)),
        dma((15,)), dma((NZ,)),
        dma((NZ,)), dma((NZ,)),
        dma((2, 8, 2)), dma((2, 8, 2)),
        dma((2, 8)), dma((2, 8)),
        dma((2,)), dma((2,)),
        dma((4,)), dma((WIN,)), dma((WIN, 2)), dma((WIN, 2, 2)),
        dma((2, 3, 8)), dma((NZ + 1,)), dma((4, NZ)),
        dma((8,)), dma((8,)),
        dma((8,)), dma((2, 4)),
        dma, dma,
    ]
    anywhere = pl.BlockSpec(memory_space=pl.ANY)
    return pl.pallas_call(
        body,
        name="attention_block",
        out_shape=jax.ShapeDtypeStruct((TB, WIDTH), BF),
        in_specs=[anywhere] * 6 + [pl.BlockSpec(memory_space=pltpu.SMEM)],
        out_specs=pl.BlockSpec(memory_space=pltpu.VMEM),
        scratch_shapes=scratch,
        compiler_params=pltpu.CompilerParams(collective_id=0, has_side_effects=True, vmem_limit_bytes=48 * 2**20),
        cost_estimate=pl.CostEstimate(flops=3 * 10**9, bytes_accessed=3 * 10**6, transcendentals=10**6),
    )(hidden_in, norm_gain.reshape(1, WIDTH), w_query, w_key, w_value, w_out, seg_lengths)


def solution(mesh):
    in_specs = (P("gy", "gx"), P("gx"), P("gx", "gy"), P("gx", None), P("gx", None), P("gy", "gx"), P())
    return jax.shard_map(shards, mesh=mesh, in_specs=in_specs, out_specs=P("gy", "gx"), check_vma=False)
```

```python
import math

import jax
import jax.numpy as jnp
from jax import lax
from jax.experimental import pallas as pl
from jax.experimental.pallas import tpu as pltpu
from jax.sharding import PartitionSpec as P

MESH = pl.DeviceIdType.MESH
HD = 128
HALF = HD // 2
SEGS = 8
ROPE_BASE = 500000.0
EPS = 1e-05
BF = jnp.bfloat16
F32 = jnp.float32

NZ = 16
TB = 128
TH = 64
WIDTH = 512
QW = 256
COLS = HD + WIDTH
WIN = 5
KEYS = WIN * TB
MODEL = 16384


def body(h, gain, wq, wk, wv, wo, seg, out, *s):
    (
        gath, wraw, kvraw, wcat, wov, gv, segs, part, zk, zkr, zq, zqr, sq, sqs, sqr, kvw, att, cs, cr, own, es, er, el, xs, xr,
        in_sem, ga_s, ga_r, gc_r, w_s, w_r, zk_s, zk_r, zq_s, zq_r, q_s, q_r, k_s, k_r, kc_r, d_s, d_r, c_s, c_r, e_s, e_r, x_s, x_r,
    ) = s
    gx = lax.axis_index("gx")
    gy = lax.axis_index("gy")
    xlo, z = lax.div(gx, NZ), lax.rem(gx, NZ)
    xhi, y, core = lax.div(gy, 8), lax.rem(lax.div(gy, 2), 4), lax.rem(gy, 2)
    xot, hot, cot = 1 - xlo, 1 - xhi, 1 - core

    def zm(v):
        return lax.rem(v + NZ, NZ)

    def ym(v):
        return lax.rem(v + 4, 4)

    def at_z(d):
        return {"gx": xlo * NZ + zm(z + d), "gy": gy}

    def at_y(yy):
        return {"gx": gx, "gy": xhi * 8 + yy * 2 + core}

    def blk(hh, yy, cc):
        return hh * 8 + yy * 2 + cc

    far = blk(hot, y, core)
    dev_x = {"gx": xot * NZ + z, "gy": gy}
    dev_h = {"gx": gx, "gy": far}
    dev_d = {"gx": xot * NZ + z, "gy": far}
    dev_c = {"gx": gx, "gy": blk(xhi, y, cot)}

    def rc(src, dst, ss, rs, dev):
        return pltpu.make_async_remote_copy(src_ref=src, dst_ref=dst, send_sem=ss, recv_sem=rs, device_id=dev, device_id_type=MESH)

    barrier = pltpu.get_barrier_semaphore()
    greet = [dev_x, dev_h, dev_d, dev_c] + [at_y(ym(y + d)) for d in (1, 2, 3)] + [at_z(d) for d in (1, 2, 3, 4, -1, -2, -3, -4)]
    for d in greet:
        pl.semaphore_signal(barrier, inc=1, device_id=d, device_id_type=MESH)
    is_core0 = core == 0
    head = pl.multiple_of((xhi * 4 + y) * HD, HD)
    mine = pl.ds(pl.multiple_of(xlo * TH, TH), TH)
    other = pl.ds(pl.multiple_of(xot * TH, TH), TH)
    loads = [
        pltpu.make_async_copy(h.at[mine], gath.at[gy, 0], in_sem.at[0]),
        pltpu.make_async_copy(wq, wraw.at[0], in_sem.at[1]),
        pltpu.make_async_copy(wo, wov.at[0], in_sem.at[2]),
        pltpu.make_async_copy(gain, gv.at[0], in_sem.at[3]),
        pltpu.make_async_copy(seg, segs, in_sem.at[4]),
    ]
    for c in loads:
        c.start()

    def kv_load(src):
        return pltpu.make_async_copy(src.at[:, pl.ds(head, HD)], kvraw.at[0], in_sem.at[5])

    def kv_send(src):
        return rc(src.at[:, pl.ds(head, HD)], kvraw.at[1], w_s.at[0], w_r.at[0], dev_x)

    @pl.when(is_core0)
    def _():
        kv_load(wk).start()

    @pl.when(core == 1)
    def _():
        kv_load(wv).start()

    pl.semaphore_wait(barrier, len(greet))

    def g_copy(dst, n, dev, src=None):
        return rc(dst if src is None else src, dst, ga_s, ga_r.at[n], dev)

    def gc_copy(ref):
        return rc(ref, ref, ga_s, gc_r, dev_c)

    ys = (1, 3, 2)
    at = {1: 4, 3: 1, 2: 7}
    by = {1: 1, 3: 4, 2: 7}
    g_copy(gath.at[gy, 1], 0, dev_x, h.at[other]).start()
    g_copy(gath.at[gy, 0], 10, dev_h, h.at[mine]).start()
    g_copy(gath.at[gy, 1], 11, dev_d, h.at[other]).start()
    for d in ys:
        g_copy(gath.at[gy, 0], at[d], at_y(ym(y + d)), h.at[mine]).start()

    @pl.when(is_core0)
    def _():
        kv_send(wk).start()

    @pl.when(core == 1)
    def _():
        kv_send(wv).start()

    cp_g = rc(gain, gv.at[1], w_s.at[1], w_r.at[1], dev_x)
    cp_q = rc(wq, wraw.at[1], w_s.at[2], w_r.at[2], dev_x)
    cp_o = rc(wo, wov.at[1], w_s.at[3], w_r.at[3], dev_x)
    cp_g.start()
    cp_q.start()
    rc(h.at[mine], gath.at[gy, 0], ga_s, gc_r, dev_c).start()

    for c in loads:
        c.wait()
    kv_load(wk).wait()

    def weights(f):
        col = jnp.transpose(jnp.broadcast_to(gv[f], (HD, WIDTH)))
        wcat[f, :, 0:HD] = (kvraw[f].astype(F32) * col).astype(BF)
        for j in range(WIDTH // HD):
            wcat[f, :, HD * (j + 1) : HD * (j + 2)] = (wraw[f, :, HD * j : HD * (j + 1)].astype(F32) * col).astype(BF)

    g_copy(gath.at[gy, 1], 0, dev_x).wait_recv()
    for d in ys:
        g_copy(gath.at[gy, 1], at[d] + 1, at_y(ym(y + d))).start()
    gc_copy(gath.at[gy, 1]).start()
    g_copy(gath.at[far, 0], 10, dev_h).wait_recv()
    g_copy(gath.at[far, 1], 11, dev_d).wait_recv()
    for d in ys:
        g_copy(gath.at[far], at[d] + 2, at_y(ym(y + d))).start()
    gc_copy(gath.at[far]).start()
    weights(0)

    def firsts(tq):
        start = jnp.zeros_like(tq)
        total = jnp.int32(0)
        for i in range(SEGS):
            start = jnp.where(tq >= total, total, start)
            total = total + segs[i]
        return start

    here = z * TB + xlo * TH
    lane = lax.broadcasted_iota(jnp.int32, (TH, HD), 1)
    tok = here + lax.broadcasted_iota(jnp.int32, (TH, HD), 0)
    pos = (tok - firsts(tok)).astype(F32)
    freq = jnp.exp((lax.rem(lane, HALF)).astype(F32) * (-2.0 / HD * math.log(ROPE_BASE)))
    angle = pos * freq
    cosine = jnp.cos(angle)
    sine = jnp.sin(angle)
    sine = jnp.where(lane < HALF, -sine, sine)

    def rotated(v):
        return v * cosine + pltpu.roll(v, HALF, 1) * sine

    for d in ys:
        b = blk(xhi, ym(y + d), core)
        g_copy(gath.at[b, 0], by[d], dev_c).wait_recv()
        g_copy(gath.at[b, 1], by[d] + 1, dev_c).wait_recv()
        gc_copy(gath.at[b]).start()
    for d in ys:
        b = blk(hot, ym(y + d), core)
        g_copy(gath.at[b], by[d] + 2, dev_c).wait_recv()
        gc_copy(gath.at[b]).start()
    rc(kvraw.at[0], kvraw.at[1], w_s.at[0], w_r.at[0], dev_x).wait_recv()
    cp_g.wait_recv()
    cp_q.wait_recv()
    cp_o.start()
    weights(1)
    gc_copy(gath.at[pl.ds(0, 8)]).wait_recv()

    ones = jnp.ones((8, WIDTH), BF)
    nt = (((1,), (1,)), ((), ()))

    def product(i):
        bp, bm = zm(z + 8 - i), zm(z - 7 + i)
        res = jnp.zeros((TB, COLS), F32)
        sums = jnp.zeros((8, TB), F32)
        for f in range(2):
            x = jnp.concatenate([gath[bp, f], gath[bm, f]], axis=0)
            res = res + jnp.dot(x, wcat[f], preferred_element_type=F32)
            xf = x.astype(F32)
            x2 = xf * xf
            hi = x2.astype(BF)
            lo = (x2 - hi.astype(F32)).astype(BF)
            sums = sums + lax.dot_general(ones, hi, nt, preferred_element_type=F32) + lax.dot_general(ones, lo, nt, preferred_element_type=F32)
        part[i] = res
        sq[i, 0] = sums
        sq[i, 1] = pltpu.roll(sums, TH, 1)

    def k_ring(d, k):
        return rc(zk.at[d, k], zkr.at[d, k], zk_s.at[d], zk_r.at[d, k], at_z(1 - 2 * d))

    def q_ring(d, k, p):
        return rc(zq.at[d, k, p], zqr.at[d, k, p], zq_s.at[d], zq_r.at[d, k, p], at_z(1 - 2 * d))

    def s_ring(d, k):
        return rc(sqs.at[d, k], sqr.at[d, k], q_s.at[d], q_r.at[d, k], at_z(1 - 2 * d))

    def mix(k, first, later):
        @pl.when(k == 0)
        def _():
            first()

        @pl.when(k > 0)
        def _():
            later()

    def send_kv(d, k):
        rows = slice(d * TH, d * TH + TH)

        def first():
            zk[d, k] = part[k, rows, 0:HD].astype(BF)

        def later():
            k_ring(d, k - 1).wait_recv()
            zk[d, k] = (part[k, rows, 0:HD] + zkr[d, k - 1].astype(F32)).astype(BF)

        mix(k, first, later)
        k_ring(d, k).start()

    def send_q(d, k, p):
        rows = slice(d * TH, d * TH + TH)
        cols = slice(HD + p * QW, HD + p * QW + QW)

        def first():
            zq[d, k, p] = part[k, rows, cols].astype(BF)

        def later():
            q_ring(d, k - 1, p).wait_recv()
            zq[d, k, p] = (part[k, rows, cols] + zqr[d, k - 1, p].astype(F32)).astype(BF)

        mix(k, first, later)
        q_ring(d, k, p).start()

    def send_sq(d, k):
        def first():
            sqs[d, k] = sq[k, d]

        def later():
            s_ring(d, k - 1).wait_recv()
            sqs[d, k] = sq[k, d] + sqr[d, k - 1]

        mix(k, first, later)
        s_ring(d, k).start()

    def ring_dir(d, k):
        send_kv(d, k)
        for p in range(2):
            send_q(d, k, p)
        send_sq(d, k)

    product(0)

    def reduce_step(k, _):
        ring_dir(0, k)

        @pl.when(k < 7)
        def _():
            ring_dir(1, k)
            product(k + 1)

        return 0

    lax.fori_loop(0, 8, reduce_step, 0)

    s_ring(0, 7).wait_recv()
    s_ring(1, 6).wait_recv()
    squares = (sq[7, 1] + sqr[0, 7] + sqr[1, 6])[0:1]
    squares = jnp.transpose(jnp.broadcast_to(squares, (HD, TB)))[0:TH]
    scale = lax.rsqrt(squares / MODEL + EPS)

    def k_copy(d, xx, n, dev, dd=None):
        to = d if dd is None else dd
        return rc(kvw.at[core, d, xx], kvw.at[core, to, xx], k_s, k_r.at[to, n], dev)

    def kc_copy(d, xx):
        return rc(kvw.at[core, d, xx], kvw.at[core, d, xx], k_s, kc_r, dev_c)

    k_ring(0, 7).wait_recv()
    k_ring(1, 6).wait_recv()
    kv = (part[7, TH:TB, 0:HD] + zkr[0, 7].astype(F32) + zkr[1, 6].astype(F32)) * scale
    kvw[core, 0, xlo] = jnp.where(is_core0, rotated(kv), kv).astype(BF)
    for d in range(WIN - 1, 0, -1):
        k_copy(0, xlo, 0, at_z(d), d).start()
    k_copy(0, xlo, 1, dev_x).start()
    kc_copy(0, xlo).start()

    queries = []
    for p in range(2):
        q_ring(0, 7, p).wait_recv()
        q_ring(1, 6, p).wait_recv()
        t = part[7, TH:TB, HD + p * QW : HD + p * QW + QW] + zqr[0, 7, p].astype(F32) + zqr[1, 6, p].astype(F32)
        for j in range(2):
            queries.append(rotated(t[:, HD * j : HD * (j + 1)] * scale).astype(BF))
    queries = jnp.concatenate(queries, axis=0)

    for d in range(1, WIN):
        k_copy(d, xlo, 0, dev_x).wait_recv()
        k_copy(d, xlo, 1, dev_x).start()
        kc_copy(d, xlo).start()
    for d in range(WIN):
        k_copy(d, xot, 1, dev_x).wait_recv()
        kc_copy(d, xot).start()
    rc(kvw.at[cot], kvw.at[cot], k_s, kc_r, dev_c).wait_recv()

    keys = kvw[0].reshape(KEYS, HD)
    values = kvw[1].reshape(KEYS, HD)
    scores = lax.dot_general(queries, keys, nt, preferred_element_type=F32) * (1.0 / math.sqrt(HD))
    n = lax.broadcasted_iota(jnp.int32, (TH, KEYS), 1)
    tk = z * TB + n - 2 * TB * lax.div(n, TB)
    tq = here + lax.broadcasted_iota(jnp.int32, (TH, KEYS), 0)
    allowed = (tk >= firsts(tq)) & (tk <= tq)

    def d_copy(d, b, p):
        return rc(att.at[b, p], att.at[b, p], d_s.at[d], d_r.at[b, p], at_z(1 - 2 * d))

    for j in range(4):
        sc = jnp.where(allowed, scores[TH * j : TH * (j + 1)], -1e30)
        e = jnp.exp(sc - jnp.max(sc, axis=1, keepdims=True))
        e = jnp.where(allowed, e, 0.0)
        o = jnp.dot(e.astype(BF), values, preferred_element_type=F32) / jnp.sum(e, axis=1, keepdims=True)
        att[z, j // 2, :, HD * (j % 2) : HD * (j % 2 + 1)] = o.astype(BF)
        if j % 2:
            for d in range(2):
                d_copy(d, z, j // 2).start()
    cp_o.wait_recv()

    def pass_on(d, k, b, last):
        for p in range(2):
            d_copy(d, b, p).wait_recv()

            @pl.when(k < last)
            def _():
                d_copy(d, b, p).start()

    def c_copy(b):
        m = lax.div(b, 2)
        return rc(cs.at[m], cr.at[m], c_s, c_r.at[m], dev_c)

    def e_copy(b, yy):
        hh, m = lax.div(b, 8), lax.div(b, 2)
        return rc(es.at[m], er.at[hh, y], e_s, e_r.at[hh, y], at_y(yy))

    def out_product(blocks):
        halves = [jnp.concatenate([att[b, p] for b in blocks], axis=0) for p in range(2)]
        for g in range(2):
            t = sum(jnp.dot(halves[p], wov[g, p * QW : p * QW + QW], preferred_element_type=F32) for p in range(2))
            cols = slice(g * WIDTH, g * WIDTH + WIDTH)
            same = lax.rem(blocks[0], 2) == core

            @pl.when(same)
            def _():
                for i, b in enumerate(blocks):
                    own[lax.div(b, 2), :, cols] = t[i * TH : i * TH + TH]

            @pl.when(jnp.logical_not(same))
            def _():
                for i, b in enumerate(blocks):
                    cs[lax.div(b, 2), :, cols] = t[i * TH : i * TH + TH].astype(BF)

        @pl.when(lax.rem(blocks[0], 2) != core)
        def _():
            for b in blocks:
                c_copy(b).start()

    def out_send(b):
        @pl.when(lax.rem(b, 2) == core)
        def _():
            m = lax.div(b, 2)
            c_copy(b).wait_recv()
            t = own[m] + cr[m].astype(F32)
            yb = lax.rem(m, 4)

            @pl.when(yb == y)
            def _():
                el[lax.div(b, 8)] = t

            @pl.when(yb != y)
            def _():
                es[m] = t.astype(BF)
                e_copy(b, yb).start()

    def gather_step(k, _):
        pass_on(0, k, zm(z - k), 8)

        @pl.when(k < 8)
        def _():
            pass_on(1, k, zm(z + k), 7)

        @pl.when(k == 1)
        def _():
            out_product([z])

        @pl.when(k > 1)
        def _():
            out_product([zm(z - k + 1), zm(z + k - 1)])
            out_send(zm(z - k + 2))

        @pl.when(k > 2)
        def _():
            out_send(zm(z + k - 2))

        return 0

    lax.fori_loop(1, 9, gather_step, 0)
    out_product([zm(z - 8)])
    out_send(zm(z - 7))
    out_send(zm(z + 7))
    out_send(zm(z - 8))

    def y_sum(hh):
        t = el[hh]
        for d in ys:
            yy = ym(y + d)
            rc(es.at[0], er.at[hh, yy], e_s, e_r.at[hh, yy], at_y(yy)).wait_recv()
            t = t + er[hh, yy].astype(F32)
        return t

    def x_copy(n, dev):
        return rc(xs.at[n], xr.at[n], x_s, x_r.at[n], dev)

    away = y_sum(hot)
    xs[0] = away[:, 0:WIDTH].astype(BF)
    x_copy(0, dev_h).start()
    xs[1] = away[:, WIDTH:].astype(BF)
    x_copy(1, dev_d).start()
    home = y_sum(xhi)
    xs[2] = home[:, WIDTH:].astype(BF)
    x_copy(2, dev_x).start()
    x_copy(0, dev_h).wait_recv()
    out[mine, :] = (home[:, 0:WIDTH] + xr[0].astype(F32)).astype(BF)
    x_copy(1, dev_d).wait_recv()
    x_copy(2, dev_x).wait_recv()
    out[other, :] = (xr[1].astype(F32) + xr[2].astype(F32)).astype(BF)

    def left(ref, sem):
        rc(ref, ref, sem, x_r.at[0], dev_x).wait_send()

    pieces = gath.reshape(2 * NZ, TH, WIDTH)
    left(pieces.at[pl.ds(0, 31)], ga_s)
    left(kvraw.at[0], w_s.at[0])
    cp_g.wait_send()
    cp_q.wait_send()
    cp_o.wait_send()
    for d in range(2):
        left(zk.at[d, pl.ds(0, 8 - d)], zk_s.at[d])
        left(zq.at[d, pl.ds(0, 8 - d)], zq_s.at[d])
        left(sqs.at[d, pl.ds(0, 8 - d)], q_s.at[d])
        left(att.at[pl.ds(0, 8 - d)], d_s.at[d])
    left(kvw.reshape(4 * WIN, TH, HD).at[pl.ds(0, 4 * WIN - 1)], k_s)
    left(cs, c_s)
    left(es.at[pl.ds(0, 6)], e_s)
    left(xs, x_s)


def shards(hidden_in, norm_gain, w_query, w_key, w_value, w_out, seg_lengths):
    v = pltpu.VMEM
    dma = pltpu.SemaphoreType.DMA
    scratch = [
        v((NZ, 2, TH, WIDTH), BF),
        v((2, WIDTH, WIDTH), BF),
        v((2, WIDTH, HD), BF),
        v((2, WIDTH, COLS), BF),
        v((2, WIDTH, WIDTH), BF),
        v((2, 1, WIDTH), F32),
        pltpu.SMEM((SEGS,), jnp.int32),
        v((8, TB, COLS), F32),
        v((2, 8, TH, HD), BF),
        v((2, 8, TH, HD), BF),
        v((2, 8, 2, TH, QW), BF),
        v((2, 8, 2, TH, QW), BF),
        v((8, 2, 8, TB), F32),
        v((2, 8, 8, TB), F32),
        v((2, 8, 8, TB), F32),
        v((2, WIN, 2, TH, HD), BF),
        v((NZ, 2, TH, QW), BF),
        v((8, TH, 2 * WIDTH), BF),
        v((8, TH, 2 * WIDTH), BF),
        v((8, TH, 2 * WIDTH), F32),
        v((8, TH, 2 * WIDTH), BF),
        v((2, 4, TH, 2 * WIDTH), BF),
        v((2, TH, 2 * WIDTH), F32),
        v((3, TH, WIDTH), BF),
        v((3, TH, WIDTH), BF),
        dma((6,)),
        dma, dma((12,)), dma,
        dma((4,)), dma((4,)),
        dma((2,)), dma((2, 8)),
        dma((2,)), dma((2, 8, 2)),
        dma((2,)), dma((2, 8)),
        dma, dma((WIN, 2)), dma,
        dma((2,)), dma((NZ, 2)),
        dma, dma((8,)),
        dma, dma((2, 4)),
        dma, dma((3,)),
    ]
    anywhere = pl.BlockSpec(memory_space=pl.ANY)
    return pl.pallas_call(
        body,
        name="attention_block",
        out_shape=jax.ShapeDtypeStruct((TB, WIDTH), BF),
        in_specs=[anywhere] * 7,
        out_specs=pl.BlockSpec(memory_space=pltpu.VMEM),
        scratch_shapes=scratch,
        compiler_params=pltpu.CompilerParams(collective_id=0, has_side_effects=True, vmem_limit_bytes=62 * 2**20),
        cost_estimate=pl.CostEstimate(flops=3 * 10**9, bytes_accessed=3 * 10**6, transcendentals=10**6),
    )(hidden_in, norm_gain.reshape(1, WIDTH), w_query, w_key, w_value, w_out, seg_lengths)


def solution(mesh):
    in_specs = (P("gy", "gx"), P("gx"), P("gx", "gy"), P("gx", None), P("gx", None), P("gy", "gx"), P())
    return jax.shard_map(shards, mesh=mesh, in_specs=in_specs, out_specs=P("gy", "gx"), check_vma=False)
```

```python
import math

import jax
import jax.numpy as jnp
from jax import lax
from jax.experimental import pallas as pl
from jax.experimental.pallas import tpu as pltpu
from jax.sharding import PartitionSpec as P

MESH = pl.DeviceIdType.MESH
HD = 128
HALF = HD // 2
SEGS = 8
ROPE_BASE = 500000.0
EPS = 1e-05
BF = jnp.bfloat16
F32 = jnp.float32

NZ = 16
TB = 128
TH = 64
WIDTH = 512
QW = 256
COLS = HD + WIDTH
JK = 4
JQ = 3
WIN = 5
KEYS = WIN * TB
MODEL = 16384


def body(h, gain, wq, wk, wv, wo, seg, out, *s):
    (
        gath, wraw, kvraw, wcat, wov, gv, segs, part, kvp, zk, zkr, zq, zqr, sqp, sqs, sqr, kvw, att, cs, cr, own, es, er, el, xs, xr,
        in_sem, ga_s, ga_r, gc_r, w_s, w_r, zk_s, zk_r, zq_s, zq_r, q_s, q_r, k_s, k_r, kc_r, d_s, d_r, c_s, c_r, e_s, e_r, x_s, x_r,
    ) = s
    gx = lax.axis_index("gx")
    gy = lax.axis_index("gy")
    xlo, z = lax.div(gx, NZ), lax.rem(gx, NZ)
    xhi, y, core = lax.div(gy, 8), lax.rem(lax.div(gy, 2), 4), lax.rem(gy, 2)
    xot, hot, cot = 1 - xlo, 1 - xhi, 1 - core

    def zm(v):
        return lax.rem(v + NZ, NZ)

    def ym(v):
        return lax.rem(v + 4, 4)

    def at_z(d):
        return {"gx": xlo * NZ + zm(z + d), "gy": gy}

    def at_y(yy):
        return {"gx": gx, "gy": xhi * 8 + yy * 2 + core}

    def blk(hh, yy, cc):
        return hh * 8 + yy * 2 + cc

    far = blk(hot, y, core)
    dev_x = {"gx": xot * NZ + z, "gy": gy}
    dev_h = {"gx": gx, "gy": far}
    dev_d = {"gx": xot * NZ + z, "gy": far}
    dev_c = {"gx": gx, "gy": blk(xhi, y, cot)}

    def rc(src, dst, ss, rs, dev):
        return pltpu.make_async_remote_copy(src_ref=src, dst_ref=dst, send_sem=ss, recv_sem=rs, device_id=dev, device_id_type=MESH)

    barrier = pltpu.get_barrier_semaphore()
    greet = [dev_x, dev_h, dev_d, dev_c] + [at_y(ym(y + d)) for d in (1, 2, 3)] + [at_z(d) for d in (1, 2, 3, 4, -1, -2, -3, -4)]
    for d in greet:
        pl.semaphore_signal(barrier, inc=1, device_id=d, device_id_type=MESH)
    is_core0 = core == 0
    head = pl.multiple_of((xhi * 4 + y) * HD, HD)
    mine = pl.ds(pl.multiple_of(xlo * TH, TH), TH)
    other = pl.ds(pl.multiple_of(xot * TH, TH), TH)
    loads = [
        pltpu.make_async_copy(h.at[mine], gath.at[gy, 0], in_sem.at[0]),
        pltpu.make_async_copy(wq, wraw.at[0], in_sem.at[1]),
        pltpu.make_async_copy(wo, wov.at[0], in_sem.at[2]),
        pltpu.make_async_copy(gain, gv.at[0], in_sem.at[3]),
        pltpu.make_async_copy(seg, segs, in_sem.at[4]),
    ]
    for c in loads:
        c.start()

    def kv_load(src):
        return pltpu.make_async_copy(src.at[:, pl.ds(head, HD)], kvraw.at[0], in_sem.at[5])

    def kv_send(src):
        return rc(src.at[:, pl.ds(head, HD)], kvraw.at[1], w_s.at[0], w_r.at[0], dev_x)

    @pl.when(is_core0)
    def _():
        kv_load(wk).start()

    @pl.when(core == 1)
    def _():
        kv_load(wv).start()

    pl.semaphore_wait(barrier, len(greet))

    def g_copy(dst, n, dev, src=None):
        return rc(dst if src is None else src, dst, ga_s, ga_r.at[n], dev)

    def gc_copy(ref):
        return rc(ref, ref, ga_s, gc_r, dev_c)

    ys = (1, 3, 2)
    at = {1: 4, 3: 1, 2: 7}
    by = {1: 1, 3: 4, 2: 7}
    g_copy(gath.at[gy, 1], 0, dev_x, h.at[other]).start()
    g_copy(gath.at[gy, 0], 10, dev_h, h.at[mine]).start()
    g_copy(gath.at[gy, 1], 11, dev_d, h.at[other]).start()
    for d in ys:
        g_copy(gath.at[gy, 0], at[d], at_y(ym(y + d)), h.at[mine]).start()

    cp_g = rc(gain, gv.at[1], w_s.at[1], w_r.at[1], dev_x)
    cp_q = rc(wq, wraw.at[1], w_s.at[2], w_r.at[2], dev_x)
    cp_o = rc(wo, wov.at[1], w_s.at[3], w_r.at[3], dev_x)
    cp_g.start()
    rc(h.at[mine], gath.at[gy, 0], ga_s, gc_r, dev_c).start()

    for c in loads:
        c.wait()
    kv_load(wk).wait()

    def gain_column(f):
        return jnp.transpose(jnp.broadcast_to(gv[f], (HD, WIDTH)))

    def kv_weights(f):
        wcat[f, :, 0:HD] = (kvraw[f].astype(F32) * gain_column(f)).astype(BF)

    def q_weights(f):
        col = gain_column(f)
        for j in range(WIDTH // HD):
            wcat[f, :, HD * (j + 1) : HD * (j + 2)] = (wraw[f, :, HD * j : HD * (j + 1)].astype(F32) * col).astype(BF)

    g_copy(gath.at[gy, 1], 0, dev_x).wait_recv()
    for d in ys:
        g_copy(gath.at[gy, 1], at[d] + 1, at_y(ym(y + d))).start()
    gc_copy(gath.at[gy, 1]).start()
    g_copy(gath.at[far, 0], 10, dev_h).wait_recv()
    g_copy(gath.at[far, 1], 11, dev_d).wait_recv()
    for d in ys:
        g_copy(gath.at[far], at[d] + 2, at_y(ym(y + d))).start()
    gc_copy(gath.at[far]).start()
    @pl.when(is_core0)
    def _():
        kv_send(wk).start()

    @pl.when(core == 1)
    def _():
        kv_send(wv).start()

    cp_q.start()
    kv_weights(0)
    q_weights(0)

    def firsts(tq):
        start = jnp.zeros_like(tq)
        total = jnp.int32(0)
        for i in range(SEGS):
            start = jnp.where(tq >= total, total, start)
            total = total + segs[i]
        return start

    here = z * TB + xlo * TH
    lane = lax.broadcasted_iota(jnp.int32, (TH, HD), 1)
    tok = here + lax.broadcasted_iota(jnp.int32, (TH, HD), 0)
    pos = (tok - firsts(tok)).astype(F32)
    freq = jnp.exp((lax.rem(lane, HALF)).astype(F32) * (-2.0 / HD * math.log(ROPE_BASE)))
    angle = pos * freq
    cosine = jnp.cos(angle)
    sine = jnp.sin(angle)
    sine = jnp.where(lane < HALF, -sine, sine)

    def rotated(v):
        return v * cosine + pltpu.roll(v, HALF, 1) * sine

    for d in ys:
        b = blk(xhi, ym(y + d), core)
        g_copy(gath.at[b, 0], by[d], dev_c).wait_recv()
        g_copy(gath.at[b, 1], by[d] + 1, dev_c).wait_recv()
        gc_copy(gath.at[b]).start()
    for d in ys:
        b = blk(hot, ym(y + d), core)
        g_copy(gath.at[b], by[d] + 2, dev_c).wait_recv()
        gc_copy(gath.at[b]).start()
    rc(kvraw.at[0], kvraw.at[1], w_s.at[0], w_r.at[0], dev_x).wait_recv()
    cp_g.wait_recv()
    kv_weights(1)
    gc_copy(gath.at[pl.ds(0, 8)]).wait_recv()

    ones = jnp.ones((8, WIDTH), BF)
    nt = (((1,), (1,)), ((), ()))

    def steps(j):
        heads = [(0, 8), (0, j - 1), (1, 7), (1, j - 1)]
        ends = [j, 1, j, 1]
        return [[(d, n - t) for (d, n), e in zip(heads, ends) if n - t >= e] for t in range(9 - j)]

    def target(d, n):
        return zm(z + (1 - 2 * d) * n)

    def leg(d, n, j):
        return at_z((1 - 2 * d) * (j if n == j else 1))

    def k_ring(d, n):
        return rc(zk.at[d, n], zkr.at[d, n], zk_s.at[d], zk_r.at[d, n], leg(d, n, JK))

    def q_ring(d, n):
        return rc(zq.at[d, n], zqr.at[d, n], zq_s.at[d], zq_r.at[d, n], leg(d, n, JQ))

    def s_ring(d, n):
        return rc(sqs.at[d, n], sqr.at[d, n], q_s.at[d], q_r.at[d, n], leg(d, n, JK))

    def add_on(d, n, j, mine, ring, stage, got):
        t = mine
        if n + 1 <= 8 - d and n + 1 != j:
            ring(d, n + 1).wait_recv()
            t = t + got[d, n + 1].astype(F32)
        stage[d, n] = t.astype(stage.dtype)
        ring(d, n).start()

    def total(j, mine, ring, got):
        t = mine
        for d in range(2):
            for n in (1, j):
                ring(d, n).wait_recv()
                t = t + got[d, n].astype(F32)
        return t

    def rows_of(pairs, f):
        return jnp.concatenate([gath[target(d, n), f] for d, n in pairs], axis=0)

    def q_product(pairs):
        res = sum(jnp.dot(rows_of(pairs, f), wcat[f, :, HD:], preferred_element_type=F32) for f in range(2))
        for i, (d, n) in enumerate(pairs):
            part[d, n] = res[i * TH : i * TH + TH]

    def sq_product(pairs):
        r = jnp.zeros((8, len(pairs) * TH), F32)
        for f in range(2):
            xf = rows_of(pairs, f).astype(F32)
            x2 = xf * xf
            hi = x2.astype(BF)
            lo = (x2 - hi.astype(F32)).astype(BF)
            r = r + lax.dot_general(ones, hi, nt, preferred_element_type=F32) + lax.dot_general(ones, lo, nt, preferred_element_type=F32)
        for i, (d, n) in enumerate(pairs):
            m = i // 2 * TB
            t = r[:, m : m + TB]
            sqp[d, n] = pltpu.roll(t, TH, 1) if i % 2 else t

    def k_step(pairs):
        for d, n in pairs:
            add_on(d, n, JK, kvp[target(d, n)], k_ring, zk, zkr)

    def s_step(pairs):
        for d, n in pairs:
            add_on(d, n, JK, sqp[d, n], s_ring, sqs, sqr)

    def q_step(pairs):
        for d, n in pairs:
            add_on(d, n, JQ, part[d, n], q_ring, zq, zqr)

    me = (0, 0)
    k_steps, q_steps = steps(JK), steps(JQ)
    kvp[...] = sum(
        jnp.dot(gath[:, f].reshape(NZ * TH, WIDTH), wcat[f, :, 0:HD], preferred_element_type=F32) for f in range(2)
    ).reshape(NZ, TH, HD)
    k_step(k_steps[0])
    sq_product(k_steps[0])
    s_step(k_steps[0])
    cp_q.wait_recv()
    cp_o.start()
    q_weights(1)
    q_product(q_steps[0])
    q_step(q_steps[0])
    for t in range(1, len(q_steps)):
        last = t == len(q_steps) - 1
        q_product(q_steps[t] + [me] * last)
        if t < len(k_steps):
            sq_product(k_steps[t] + [me] * (len(k_steps[t]) % 2))
            k_step(k_steps[t])
            s_step(k_steps[t])
        q_step(q_steps[t])

    squares = total(JK, sqp[me], s_ring, sqr)[0:1]
    squares = jnp.transpose(jnp.broadcast_to(squares, (HD, TB)))[0:TH]
    scale = lax.rsqrt(squares / MODEL + EPS)

    def k_copy(d, xx, n, dev, dd=None):
        to = d if dd is None else dd
        return rc(kvw.at[core, d, xx], kvw.at[core, to, xx], k_s, k_r.at[to, n], dev)

    def kc_copy(d, xx):
        return rc(kvw.at[core, d, xx], kvw.at[core, d, xx], k_s, kc_r, dev_c)

    kv = total(JK, kvp[z], k_ring, zkr) * scale
    kvw[core, 0, xlo] = jnp.where(is_core0, rotated(kv), kv).astype(BF)
    for d in range(WIN - 1, 0, -1):
        k_copy(0, xlo, 0, at_z(d), d).start()
    k_copy(0, xlo, 1, dev_x).start()
    kc_copy(0, xlo).start()

    q_sum = total(JQ, part[me], q_ring, zqr)
    queries = [rotated(q_sum[:, HD * j : HD * (j + 1)] * scale).astype(BF) for j in range(4)]
    queries = jnp.concatenate(queries, axis=0)

    for d in range(1, WIN):
        k_copy(d, xlo, 0, dev_x).wait_recv()
        k_copy(d, xlo, 1, dev_x).start()
        kc_copy(d, xlo).start()
    for d in range(WIN):
        k_copy(d, xot, 1, dev_x).wait_recv()
        kc_copy(d, xot).start()
    rc(kvw.at[cot], kvw.at[cot], k_s, kc_r, dev_c).wait_recv()

    keys = kvw[0].reshape(KEYS, HD)
    values = kvw[1].reshape(KEYS, HD)
    scores = lax.dot_general(queries, keys, nt, preferred_element_type=F32) * (1.0 / math.sqrt(HD))
    n = lax.broadcasted_iota(jnp.int32, (TH, KEYS), 1)
    tk = z * TB + n - 2 * TB * lax.div(n, TB)
    tq = here + lax.broadcasted_iota(jnp.int32, (TH, KEYS), 0)
    allowed = (tk >= firsts(tq)) & (tk <= tq)

    def d_copy(d, b, p, hops=1):
        return rc(att.at[b, p], att.at[b, p], d_s.at[d], d_r.at[b, p], at_z((1 - 2 * d) * hops))

    for j in range(4):
        sc = jnp.where(allowed, scores[TH * j : TH * (j + 1)], -1e30)
        e = jnp.exp(sc - jnp.max(sc, axis=1, keepdims=True))
        e = jnp.where(allowed, e, 0.0)
        o = jnp.dot(e.astype(BF), values, preferred_element_type=F32) / jnp.sum(e, axis=1, keepdims=True)
        att[z, j // 2, :, HD * (j % 2) : HD * (j % 2 + 1)] = o.astype(BF)
        if j % 2:
            for d in range(2):
                d_copy(d, z, j // 2).start()
                d_copy(d, z, j // 2, JK).start()
    cp_o.wait_recv()

    def pass_on(d, n):
        b = zm(z - (1 - 2 * d) * n)
        for p in range(2):
            d_copy(d, b, p).wait_recv()

            @pl.when((n != JK - 1) & (n < 8 - d))
            def _():
                d_copy(d, b, p).start()

    def c_copy(b):
        m = lax.div(b, 2)
        return rc(cs.at[m], cr.at[m], c_s, c_r.at[m], dev_c)

    def e_copy(b, yy):
        hh, m = lax.div(b, 8), lax.div(b, 2)
        return rc(es.at[m], er.at[hh, y], e_s, e_r.at[hh, y], at_y(yy))

    def out_product(blocks):
        halves = [jnp.concatenate([att[b, p] for b in blocks], axis=0) for p in range(2)]
        for g in range(2):
            t = sum(jnp.dot(halves[p], wov[g, p * QW : p * QW + QW], preferred_element_type=F32) for p in range(2))
            cols = slice(g * WIDTH, g * WIDTH + WIDTH)
            same = lax.rem(blocks[0], 2) == core

            @pl.when(same)
            def _():
                for i, b in enumerate(blocks):
                    own[lax.div(b, 2), :, cols] = t[i * TH : i * TH + TH]

            @pl.when(jnp.logical_not(same))
            def _():
                for i, b in enumerate(blocks):
                    cs[lax.div(b, 2), :, cols] = t[i * TH : i * TH + TH].astype(BF)

        @pl.when(lax.rem(blocks[0], 2) != core)
        def _():
            for b in blocks:
                c_copy(b).start()

    def out_send(b):
        @pl.when(lax.rem(b, 2) == core)
        def _():
            m = lax.div(b, 2)
            c_copy(b).wait_recv()
            t = own[m] + cr[m].astype(F32)
            yb = lax.rem(m, 4)

            @pl.when(yb == y)
            def _():
                el[lax.div(b, 8)] = t

            @pl.when(yb != y)
            def _():
                es[m] = t.astype(BF)
                e_copy(b, yb).start()

    def hops(k):
        odd = lax.rem(k, 2)
        return odd * lax.div(k + 1, 2) + (1 - odd) * (JK - 1 + lax.div(k, 2))

    def both(n):
        return [zm(z - n), zm(z + n)]

    def gather_step(k, _):
        for d in range(2):
            pass_on(d, hops(k))

        @pl.when(k == 1)
        def _():
            out_product([z])

        @pl.when(k > 1)
        def _():
            out_product(both(hops(k - 1)))

        @pl.when(k == 2)
        def _():
            out_send(z)

        @pl.when(k > 2)
        def _():
            for b in both(hops(k - 2)):
                out_send(b)

        return 0

    lax.fori_loop(1, 7, gather_step, 0)
    pass_on(0, 7)
    pass_on(1, 7)
    out_product(both(6))
    for b in both(3):
        out_send(b)
    pass_on(0, 8)
    out_product(both(7))
    for b in both(6):
        out_send(b)
    out_product([zm(z - 8)])
    for b in both(7):
        out_send(b)
    out_send(zm(z - 8))

    def y_sum(hh):
        t = el[hh]
        for d in ys:
            yy = ym(y + d)
            rc(es.at[0], er.at[hh, yy], e_s, e_r.at[hh, yy], at_y(yy)).wait_recv()
            t = t + er[hh, yy].astype(F32)
        return t

    def x_copy(n, dev):
        return rc(xs.at[n], xr.at[n], x_s, x_r.at[n], dev)

    away = y_sum(hot)
    xs[0] = away[:, 0:WIDTH].astype(BF)
    x_copy(0, dev_h).start()
    xs[1] = away[:, WIDTH:].astype(BF)
    x_copy(1, dev_d).start()
    home = y_sum(xhi)
    xs[2] = home[:, WIDTH:].astype(BF)
    x_copy(2, dev_x).start()
    x_copy(0, dev_h).wait_recv()
    out[mine, :] = (home[:, 0:WIDTH] + xr[0].astype(F32)).astype(BF)
    x_copy(1, dev_d).wait_recv()
    x_copy(2, dev_x).wait_recv()
    out[other, :] = (xr[1].astype(F32) + xr[2].astype(F32)).astype(BF)

    def left(ref, sem):
        rc(ref, ref, sem, x_r.at[0], dev_x).wait_send()

    pieces = gath.reshape(2 * NZ, TH, WIDTH)
    left(pieces.at[pl.ds(0, 31)], ga_s)
    left(kvraw.at[0], w_s.at[0])
    cp_g.wait_send()
    cp_q.wait_send()
    cp_o.wait_send()
    for d in range(2):
        left(zk.at[d, pl.ds(0, 8 - d)], zk_s.at[d])
        left(zq.at[d, pl.ds(0, 8 - d)], zq_s.at[d])
        left(sqs.at[d, pl.ds(0, 8 - d)], q_s.at[d])
        left(att.at[pl.ds(0, 8 - d)], d_s.at[d])
    left(kvw.reshape(4 * WIN, TH, HD).at[pl.ds(0, 4 * WIN - 1)], k_s)
    left(cs, c_s)
    left(es.at[pl.ds(0, 6)], e_s)
    left(xs, x_s)


def shards(hidden_in, norm_gain, w_query, w_key, w_value, w_out, seg_lengths):
    v = pltpu.VMEM
    dma = pltpu.SemaphoreType.DMA
    scratch = [
        v((NZ, 2, TH, WIDTH), BF),
        v((2, WIDTH, WIDTH), BF),
        v((2, WIDTH, HD), BF),
        v((2, WIDTH, COLS), BF),
        v((2, WIDTH, WIDTH), BF),
        v((2, 1, WIDTH), F32),
        pltpu.SMEM((SEGS,), jnp.int32),
        v((2, 9, TH, WIDTH), F32),
        v((NZ, TH, HD), F32),
        v((2, 9, TH, HD), BF),
        v((2, 9, TH, HD), BF),
        v((2, 9, TH, WIDTH), BF),
        v((2, 9, TH, WIDTH), BF),
        v((2, 9, 8, TB), F32),
        v((2, 9, 8, TB), F32),
        v((2, 9, 8, TB), F32),
        v((2, WIN, 2, TH, HD), BF),
        v((NZ, 2, TH, QW), BF),
        v((8, TH, 2 * WIDTH), BF),
        v((8, TH, 2 * WIDTH), BF),
        v((8, TH, 2 * WIDTH), F32),
        v((8, TH, 2 * WIDTH), BF),
        v((2, 4, TH, 2 * WIDTH), BF),
        v((2, TH, 2 * WIDTH), F32),
        v((3, TH, WIDTH), BF),
        v((3, TH, WIDTH), BF),
        dma((6,)),
        dma, dma((12,)), dma,
        dma((4,)), dma((4,)),
        dma((2,)), dma((2, 9)),
        dma((2,)), dma((2, 9)),
        dma((2,)), dma((2, 9)),
        dma, dma((WIN, 2)), dma,
        dma((2,)), dma((NZ, 2)),
        dma, dma((8,)),
        dma, dma((2, 4)),
        dma, dma((3,)),
    ]
    anywhere = pl.BlockSpec(memory_space=pl.ANY)
    return pl.pallas_call(
        body,
        name="attention_block",
        out_shape=jax.ShapeDtypeStruct((TB, WIDTH), BF),
        in_specs=[anywhere] * 7,
        out_specs=pl.BlockSpec(memory_space=pltpu.VMEM),
        scratch_shapes=scratch,
        compiler_params=pltpu.CompilerParams(collective_id=0, has_side_effects=True, vmem_limit_bytes=62 * 2**20),
        cost_estimate=pl.CostEstimate(flops=3 * 10**9, bytes_accessed=3 * 10**6, transcendentals=10**6),
    )(hidden_in, norm_gain.reshape(1, WIDTH), w_query, w_key, w_value, w_out, seg_lengths)


def solution(mesh):
    in_specs = (P("gy", "gx"), P("gx"), P("gx", "gy"), P("gx", None), P("gx", None), P("gy", "gx"), P())
    return jax.shard_map(shards, mesh=mesh, in_specs=in_specs, out_specs=P("gy", "gx"), check_vma=False)
```

```python
import math

import jax
import jax.numpy as jnp
from jax import lax
from jax.experimental import pallas as pl
from jax.experimental.pallas import tpu as pltpu
from jax.sharding import PartitionSpec as P

MESH = pl.DeviceIdType.MESH
HD = 128
HALF = HD // 2
SEGS = 8
ROPE_BASE = 500000.0
EPS = 1e-05
BF = jnp.bfloat16
F32 = jnp.float32

NZ = 16
TB = 128
TH = 64
WIDTH = 512
QW = 256
COLS = HD + WIDTH
JK = (4,)
JQ = (3,)
JD = (5,)
ORDER = (1, 5, 2, 6, 3, 7, 4, 8)
KROWS = TH + 16
WIN = 5
KEYS = WIN * TB
MODEL = 16384


def body(h, gain, wq, wk, wv, wo, seg, out, *s):
    (
        gath, wraw, kvraw, wcat, wov, gv, segs, part, kvp, zk, zkr, zq, zqr, sqp, kvw, att, cs, cr, own, es, er, el, xs, xr,
        in_sem, ga_s, ga_r, gc_r, w_s, w_r, zk_s, zk_r, zq_s, zq_r, k_s, k_r, kc_r, d_s, d_r, c_s, c_r, e_s, e_r, x_s, x_r,
    ) = s
    gx = lax.axis_index("gx")
    gy = lax.axis_index("gy")
    xlo, z = lax.div(gx, NZ), lax.rem(gx, NZ)
    xhi, y, core = lax.div(gy, 8), lax.rem(lax.div(gy, 2), 4), lax.rem(gy, 2)
    xot, hot, cot = 1 - xlo, 1 - xhi, 1 - core

    def zm(v):
        return lax.rem(v + NZ, NZ)

    def ym(v):
        return lax.rem(v + 4, 4)

    def at_z(d, xx=None):
        return {"gx": (xlo if xx is None else xx) * NZ + zm(z + d), "gy": gy}

    def at_y(yy):
        return {"gx": gx, "gy": xhi * 8 + yy * 2 + core}

    def blk(hh, yy, cc):
        return hh * 8 + yy * 2 + cc

    far = blk(hot, y, core)
    dev_x = {"gx": xot * NZ + z, "gy": gy}
    dev_h = {"gx": gx, "gy": far}
    dev_d = {"gx": xot * NZ + z, "gy": far}
    dev_c = {"gx": gx, "gy": blk(xhi, y, cot)}

    def rc(src, dst, ss, rs, dev):
        return pltpu.make_async_remote_copy(src_ref=src, dst_ref=dst, send_sem=ss, recv_sem=rs, device_id=dev, device_id_type=MESH)

    barrier = pltpu.get_barrier_semaphore()
    greet = [dev_x, dev_h, dev_d, dev_c] + [at_y(ym(y + d)) for d in (1, 2, 3)] + [at_z(d) for d in (1, 2, 3, 4, 5, -1, -2, -3, -4, -5)]
    for d in greet:
        pl.semaphore_signal(barrier, inc=1, device_id=d, device_id_type=MESH)
    is_core0 = core == 0
    head = pl.multiple_of((xhi * 4 + y) * HD, HD)
    mine = pl.ds(pl.multiple_of(xlo * TH, TH), TH)
    other = pl.ds(pl.multiple_of(xot * TH, TH), TH)
    loads = [
        pltpu.make_async_copy(h.at[mine], gath.at[gy, 0], in_sem.at[0]),
        pltpu.make_async_copy(wq, wraw.at[0], in_sem.at[1]),
        pltpu.make_async_copy(wo, wov.at[0], in_sem.at[2]),
        pltpu.make_async_copy(gain, gv.at[0], in_sem.at[3]),
        pltpu.make_async_copy(seg, segs, in_sem.at[4]),
    ]
    for c in loads:
        c.start()

    def kv_load(src):
        return pltpu.make_async_copy(src.at[:, pl.ds(head, HD)], kvraw.at[0], in_sem.at[5])

    def kv_send(src):
        return rc(src.at[:, pl.ds(head, HD)], kvraw.at[1], w_s.at[0], w_r.at[0], dev_x)

    @pl.when(is_core0)
    def _():
        kv_load(wk).start()

    @pl.when(core == 1)
    def _():
        kv_load(wv).start()

    pl.semaphore_wait(barrier, len(greet))

    def g_copy(dst, n, dev, src=None):
        return rc(dst if src is None else src, dst, ga_s, ga_r.at[n], dev)

    def gc_copy(ref):
        return rc(ref, ref, ga_s, gc_r, dev_c)

    ys = (1, 3, 2)
    at = {1: 4, 3: 1, 2: 7}
    by = {1: 1, 3: 4, 2: 7}
    g_copy(gath.at[gy, 1], 0, dev_x, h.at[other]).start()
    g_copy(gath.at[gy, 0], 10, dev_h, h.at[mine]).start()
    g_copy(gath.at[gy, 1], 11, dev_d, h.at[other]).start()
    for d in ys:
        g_copy(gath.at[gy, 0], at[d], at_y(ym(y + d)), h.at[mine]).start()

    cp_g = rc(gain, gv.at[1], w_s.at[1], w_r.at[1], dev_x)
    cp_q = [rc(wq.at[:, pl.ds(p * QW, QW)], wraw.at[1, :, pl.ds(p * QW, QW)], w_s.at[2 + p], w_r.at[2 + p], dev_x) for p in range(2)]
    cp_o = rc(wo, wov.at[1], w_s.at[4], w_r.at[4], dev_x)
    cp_g.start()
    rc(h.at[mine], gath.at[gy, 0], ga_s, gc_r, dev_c).start()

    for c in loads:
        c.wait()
    kv_load(wk).wait()

    def gain_column(f):
        return jnp.transpose(jnp.broadcast_to(gv[f], (HD, WIDTH)))

    def kv_weights(f):
        wcat[f, :, 0:HD] = (kvraw[f].astype(F32) * gain_column(f)).astype(BF)

    def q_weights(f, p):
        col = gain_column(f)
        for j in range(2 * p, 2 * p + 2):
            wcat[f, :, HD * (j + 1) : HD * (j + 2)] = (wraw[f, :, HD * j : HD * (j + 1)].astype(F32) * col).astype(BF)

    g_copy(gath.at[gy, 1], 0, dev_x).wait_recv()
    for d in ys:
        g_copy(gath.at[gy, 1], at[d] + 1, at_y(ym(y + d))).start()
    gc_copy(gath.at[gy, 1]).start()
    g_copy(gath.at[far, 0], 10, dev_h).wait_recv()
    g_copy(gath.at[far, 1], 11, dev_d).wait_recv()
    for d in ys:
        g_copy(gath.at[far], at[d] + 2, at_y(ym(y + d))).start()
    gc_copy(gath.at[far]).start()
    @pl.when(is_core0)
    def _():
        kv_send(wk).start()

    @pl.when(core == 1)
    def _():
        kv_send(wv).start()

    cp_q[0].start()
    kv_weights(0)
    for p in range(2):
        q_weights(0, p)

    def firsts(tq):
        start = jnp.zeros_like(tq)
        total = jnp.int32(0)
        for i in range(SEGS):
            start = jnp.where(tq >= total, total, start)
            total = total + segs[i]
        return start

    here = z * TB + xlo * TH
    lane = lax.broadcasted_iota(jnp.int32, (TH, HD), 1)
    tok = here + lax.broadcasted_iota(jnp.int32, (TH, HD), 0)
    pos = (tok - firsts(tok)).astype(F32)
    freq = jnp.exp((lax.rem(lane, HALF)).astype(F32) * (-2.0 / HD * math.log(ROPE_BASE)))
    angle = pos * freq
    cosine = jnp.cos(angle)
    sine = jnp.sin(angle)
    sine = jnp.where(lane < HALF, -sine, sine)

    def rotated(v):
        return v * cosine + pltpu.roll(v, HALF, 1) * sine

    for d in ys:
        b = blk(xhi, ym(y + d), core)
        g_copy(gath.at[b, 0], by[d], dev_c).wait_recv()
        g_copy(gath.at[b, 1], by[d] + 1, dev_c).wait_recv()
        gc_copy(gath.at[b]).start()
    rc(kvraw.at[0], kvraw.at[1], w_s.at[0], w_r.at[0], dev_x).wait_recv()
    cp_q[1].start()
    cp_g.wait_recv()
    kv_weights(1)
    for d in ys:
        b = blk(hot, ym(y + d), core)
        g_copy(gath.at[b], by[d] + 2, dev_c).wait_recv()
        gc_copy(gath.at[b]).start()
    gc_copy(gath.at[pl.ds(0, 8)]).wait_recv()

    ones = jnp.ones((8, WIDTH), BF)
    nt = (((1,), (1,)), ((), ()))

    def steps(jumps):
        ends = (*jumps, 1)
        runs = [(d, top, end) for d in range(2) for top, end in zip((8 - d, *(j - 1 for j in jumps)), ends)]
        most = max(top - end for _, top, end in runs) + 1
        return [[(d, top - t) for d, top, end in runs if top - t >= end] for t in range(most)]

    def target(d, n):
        return zm(z + (1 - 2 * d) * n)

    def leg(d, n, jumps):
        return at_z((1 - 2 * d) * (n if n in jumps else 1))

    def k_ring(d, n):
        return rc(zk.at[d, n], zkr.at[d, n], zk_s.at[d], zk_r.at[d, n], leg(d, n, JK))

    def q_ring(p):
        return lambda d, n: rc(zq.at[p, d, n], zqr.at[p, d, n], zq_s.at[p, d], zq_r.at[p, d, n], leg(d, n, JQ))

    def before(d, n, jumps):
        return n + 1 <= 8 - d and n + 1 not in jumps

    def read_kv(d, n):
        k_ring(d, n).wait_recv()
        v = zkr[d, n].astype(F32)
        return v[0:TH], v[TH : TH + 8] + v[TH + 8 :]

    def total(jumps, mine, ring, got):
        t = mine
        for d in range(2):
            for n in (1, *jumps):
                ring(d, n).wait_recv()
                t = t + got[d, n].astype(F32)
        return t

    def rows_of(pairs, f):
        return jnp.concatenate([gath[target(d, n), f] for d, n in pairs], axis=0)

    def q_product(p, pairs):
        cols = slice(HD + p * QW, HD + p * QW + QW)
        res = sum(jnp.dot(rows_of(pairs, f), wcat[f, :, cols], preferred_element_type=F32) for f in range(2))
        for i, (d, n) in enumerate(pairs):
            part[p, d, n] = res[i * TH : i * TH + TH]

    def sq_product(pairs):
        r = jnp.zeros((8, len(pairs) * TH), F32)
        for f in range(2):
            xf = rows_of(pairs, f).astype(F32)
            x2 = xf * xf
            hi = x2.astype(BF)
            lo = (x2 - hi.astype(F32)).astype(BF)
            r = r + lax.dot_general(ones, hi, nt, preferred_element_type=F32) + lax.dot_general(ones, lo, nt, preferred_element_type=F32)
        for i, (d, n) in enumerate(pairs):
            m = i // 2 * TB
            t = r[:, m : m + TB]
            sqp[d, n] = pltpu.roll(t, TH, 1) if i % 2 else t

    def k_step(pairs):
        for d, n in pairs:
            t, q = kvp[target(d, n)], sqp[d, n]
            if before(d, n, JK):
                t2, q2 = read_kv(d, n + 1)
                t, q = t + t2, q + q2
            hi = q.astype(BF).astype(F32)
            zk[d, n] = jnp.concatenate([t, hi, q - hi], axis=0).astype(BF)
            k_ring(d, n).start()

    def q_step(p, pairs):
        for d, n in pairs:
            t = part[p, d, n]
            if before(d, n, JQ):
                q_ring(p)(d, n + 1).wait_recv()
                t = t + zqr[p, d, n + 1].astype(F32)
            zq[p, d, n] = t.astype(BF)
            q_ring(p)(d, n).start()

    me = (0, 0)
    k_steps, q_steps = steps(JK), steps(JQ)
    kvp[...] = sum(
        jnp.dot(gath[:, f].reshape(NZ * TH, WIDTH), wcat[f, :, 0:HD], preferred_element_type=F32) for f in range(2)
    ).reshape(NZ, TH, HD)
    sq_product(k_steps[0])
    k_step(k_steps[0])
    def k_copy(d, xx, n, dev, dd=None):
        to = d if dd is None else dd
        return rc(kvw.at[core, d, xx], kvw.at[core, to, xx], k_s, k_r.at[to, n], dev)

    def kc_copy(d, xx):
        return rc(kvw.at[core, d, xx], kvw.at[core, d, xx], k_s, kc_r, dev_c)

    def window_sends():
        kv, squares = kvp[z], sqp[me]
        for d in range(2):
            for n in (1, *JK):
                t, q = read_kv(d, n)
                kv, squares = kv + t, squares + q
        squares = jnp.transpose(jnp.broadcast_to(squares[0:1], (HD, TB)))[0:TH]
        scale = lax.rsqrt(squares / MODEL + EPS)
        kv = kv * scale
        kvw[core, 0, xlo] = jnp.where(is_core0, rotated(kv), kv).astype(BF)
        for d in range(WIN - 1, 0, -1):
            k_copy(0, xlo, 0, at_z(d), d).start()
        k_copy(0, xlo, 1, dev_x).start()
        kc_copy(0, xlo).start()
        return scale

    def queries_of(p):
        t = total(JQ, part[(p, *me)], q_ring(p), zqr.at[p])
        return [rotated(t[:, HD * j : HD * (j + 1)] * scale).astype(BF) for j in range(2)]

    lag = 1
    n_q = len(q_steps)
    for t in range(n_q + lag):
        if t == 0:
            cp_q[0].wait_recv()
            q_weights(1, 0)
        if t == lag:
            cp_q[1].wait_recv()
            cp_o.start()
            q_weights(1, 1)
        now = [(p, t - p * lag) for p in range(2) if 0 <= t - p * lag < n_q]
        for p, i in now:
            q_product(p, q_steps[i] + [me] * (i == n_q - 1))
        if 0 < t < len(k_steps):
            sq_product(k_steps[t] + [me] * (len(k_steps[t]) % 2))
            k_step(k_steps[t])
        for p, i in now:
            q_step(p, q_steps[i])
        if t == len(k_steps):
            scale = window_sends()

    queries = queries_of(0)
    k_copy(0, xot, 1, dev_x).wait_recv()
    kc_copy(0, xot).start()
    for d in range(1, WIN):
        k_copy(d, xlo, 0, dev_x).wait_recv()
        k_copy(d, xlo, 1, dev_x).start()
        kc_copy(d, xlo).start()
    for d in range(1, WIN):
        k_copy(d, xot, 1, dev_x).wait_recv()
        kc_copy(d, xot).start()
    queries = jnp.concatenate(queries + queries_of(1), axis=0)
    rc(kvw.at[cot], kvw.at[cot], k_s, kc_r, dev_c).wait_recv()

    keys = kvw[0].reshape(KEYS, HD)
    values = kvw[1].reshape(KEYS, HD)
    scores = lax.dot_general(queries, keys, nt, preferred_element_type=F32) * (1.0 / math.sqrt(HD))
    n = lax.broadcasted_iota(jnp.int32, (TH, KEYS), 1)
    tk = z * TB + n - 2 * TB * lax.div(n, TB)
    tq = here + lax.broadcasted_iota(jnp.int32, (TH, KEYS), 0)
    allowed = (tk >= firsts(tq)) & (tk <= tq)

    def d_copy(d, b, p, hops=1):
        return rc(att.at[b, p], att.at[b, p], d_s.at[d], d_r.at[b, p], at_z((1 - 2 * d) * hops))

    for j in range(4):
        sc = jnp.where(allowed, scores[TH * j : TH * (j + 1)], -1e30)
        e = jnp.exp(sc - jnp.max(sc, axis=1, keepdims=True))
        e = jnp.where(allowed, e, 0.0)
        o = jnp.dot(e.astype(BF), values, preferred_element_type=F32) / jnp.sum(e, axis=1, keepdims=True)
        att[z, j // 2, :, HD * (j % 2) : HD * (j % 2 + 1)] = o.astype(BF)
        if j % 2:
            for d in range(2):
                for hops in JD:
                    d_copy(d, z, j // 2, hops).start()
                d_copy(d, z, j // 2).start()
    cp_o.wait_recv()

    def pass_on(d, n):
        b = zm(z - (1 - 2 * d) * n)
        for p in range(2):
            d_copy(d, b, p).wait_recv()
            if n + 1 not in JD and n < 8 - d:
                d_copy(d, b, p).start()

    def c_copy(b):
        m = lax.div(b, 2)
        return rc(cs.at[m], cr.at[m], c_s, c_r.at[m], dev_c)

    def e_copy(b, yy):
        hh, m = lax.div(b, 8), lax.div(b, 2)
        return rc(es.at[m], er.at[hh, y], e_s, e_r.at[hh, y], at_y(yy))

    def out_product(blocks):
        halves = [jnp.concatenate([att[b, p] for b in blocks], axis=0) for p in range(2)]
        for g in range(2):
            t = sum(jnp.dot(halves[p], wov[g, p * QW : p * QW + QW], preferred_element_type=F32) for p in range(2))
            cols = slice(g * WIDTH, g * WIDTH + WIDTH)
            same = lax.rem(blocks[0], 2) == core

            @pl.when(same)
            def _():
                for i, b in enumerate(blocks):
                    own[lax.div(b, 2), :, cols] = t[i * TH : i * TH + TH]

            @pl.when(jnp.logical_not(same))
            def _():
                for i, b in enumerate(blocks):
                    cs[lax.div(b, 2), :, cols] = t[i * TH : i * TH + TH].astype(BF)

        @pl.when(lax.rem(blocks[0], 2) != core)
        def _():
            for b in blocks:
                c_copy(b).start()

    def out_send(b):
        @pl.when(lax.rem(b, 2) == core)
        def _():
            m = lax.div(b, 2)
            c_copy(b).wait_recv()
            t = own[m] + cr[m].astype(F32)
            yb = lax.rem(m, 4)

            @pl.when(yb == y)
            def _():
                el[lax.div(b, 8)] = t

            @pl.when(yb != y)
            def _():
                es[m] = t.astype(BF)
                e_copy(b, yb).start()

    def both(n):
        return [zm(z - n), zm(z + n)][: 1 if n in (0, 8) else 2]

    done = (0, *ORDER)
    for i in range(1, 11):
        if i < 9:
            for d in range(2 if done[i] < 8 else 1):
                pass_on(d, done[i])
        if i < 10:
            out_product(both(done[i - 1]))
        if i > 1:
            for b in both(done[i - 2]):
                out_send(b)

    def y_sum(hh):
        t = el[hh]
        for d in ys:
            yy = ym(y + d)
            rc(es.at[0], er.at[hh, yy], e_s, e_r.at[hh, yy], at_y(yy)).wait_recv()
            t = t + er[hh, yy].astype(F32)
        return t

    def x_copy(n, dev):
        return rc(xs.at[n], xr.at[n], x_s, x_r.at[n], dev)

    away = y_sum(hot)
    xs[0] = away[:, 0:WIDTH].astype(BF)
    x_copy(0, dev_h).start()
    xs[1] = away[:, WIDTH:].astype(BF)
    x_copy(1, dev_d).start()
    home = y_sum(xhi)
    xs[2] = home[:, WIDTH:].astype(BF)
    x_copy(2, dev_x).start()
    x_copy(0, dev_h).wait_recv()
    out[mine, :] = (home[:, 0:WIDTH] + xr[0].astype(F32)).astype(BF)
    x_copy(1, dev_d).wait_recv()
    x_copy(2, dev_x).wait_recv()
    out[other, :] = (xr[1].astype(F32) + xr[2].astype(F32)).astype(BF)

    def left(ref, sem):
        rc(ref, ref, sem, x_r.at[0], dev_x).wait_send()

    pieces = gath.reshape(2 * NZ, TH, WIDTH)
    left(pieces.at[pl.ds(0, 31)], ga_s)
    left(kvraw.at[0], w_s.at[0])
    cp_g.wait_send()
    for c in cp_q:
        c.wait_send()
    cp_o.wait_send()
    for d in range(2):
        left(zk.at[d, pl.ds(0, 8 - d)], zk_s.at[d])
        for p in range(2):
            left(zq.at[p, d, pl.ds(0, 8 - d)], zq_s.at[p, d])
        left(att.at[pl.ds(0, 8 - d)], d_s.at[d])
    left(kvw.reshape(4 * WIN, TH, HD).at[pl.ds(0, 4 * WIN - 1)], k_s)
    left(cs, c_s)
    left(es.at[pl.ds(0, 6)], e_s)
    left(xs, x_s)


def shards(hidden_in, norm_gain, w_query, w_key, w_value, w_out, seg_lengths):
    v = pltpu.VMEM
    dma = pltpu.SemaphoreType.DMA
    scratch = [
        v((NZ, 2, TH, WIDTH), BF),
        v((2, WIDTH, WIDTH), BF),
        v((2, WIDTH, HD), BF),
        v((2, WIDTH, COLS), BF),
        v((2, WIDTH, WIDTH), BF),
        v((2, 1, WIDTH), F32),
        pltpu.SMEM((SEGS,), jnp.int32),
        v((2, 2, 9, TH, QW), F32),
        v((NZ, TH, HD), F32),
        v((2, 9, KROWS, HD), BF),
        v((2, 9, KROWS, HD), BF),
        v((2, 2, 9, TH, QW), BF),
        v((2, 2, 9, TH, QW), BF),
        v((2, 9, 8, TB), F32),
        v((2, WIN, 2, TH, HD), BF),
        v((NZ, 2, TH, QW), BF),
        v((8, TH, 2 * WIDTH), BF),
        v((8, TH, 2 * WIDTH), BF),
        v((8, TH, 2 * WIDTH), F32),
        v((8, TH, 2 * WIDTH), BF),
        v((2, 4, TH, 2 * WIDTH), BF),
        v((2, TH, 2 * WIDTH), F32),
        v((3, TH, WIDTH), BF),
        v((3, TH, WIDTH), BF),
        dma((6,)),
        dma, dma((12,)), dma,
        dma((5,)), dma((5,)),
        dma((2,)), dma((2, 9)),
        dma((2, 2)), dma((2, 2, 9)),
        dma, dma((WIN, 2)), dma,
        dma((2,)), dma((NZ, 2)),
        dma, dma((8,)),
        dma, dma((2, 4)),
        dma, dma((3,)),
    ]
    anywhere = pl.BlockSpec(memory_space=pl.ANY)
    return pl.pallas_call(
        body,
        name="attention_block",
        out_shape=jax.ShapeDtypeStruct((TB, WIDTH), BF),
        in_specs=[anywhere] * 7,
        out_specs=pl.BlockSpec(memory_space=pltpu.VMEM),
        scratch_shapes=scratch,
        compiler_params=pltpu.CompilerParams(collective_id=0, has_side_effects=True, vmem_limit_bytes=62 * 2**20),
        cost_estimate=pl.CostEstimate(flops=3 * 10**9, bytes_accessed=3 * 10**6, transcendentals=10**6),
    )(hidden_in, norm_gain.reshape(1, WIDTH), w_query, w_key, w_value, w_out, seg_lengths)


def solution(mesh):
    in_specs = (P("gy", "gx"), P("gx"), P("gx", "gy"), P("gx", None), P("gx", None), P("gy", "gx"), P())
    return jax.shard_map(shards, mesh=mesh, in_specs=in_specs, out_specs=P("gy", "gx"), check_vma=False)
```

```python
import math

import jax
import jax.numpy as jnp
from jax import lax
from jax.experimental import pallas as pl
from jax.experimental.pallas import tpu as pltpu
from jax.sharding import PartitionSpec as P

MESH = pl.DeviceIdType.MESH
HD = 128
HALF = HD // 2
SEGS = 8
ROPE_BASE = 500000.0
EPS = 1e-05
BF = jnp.bfloat16
F32 = jnp.float32

NZ = 16
TB = 128
TH = 64
WIDTH = 512
QW = 256
COLS = HD + WIDTH
JK = (5,)
JQ = (4,)
JD = (5,)
ORDER = (1, 5, 2, 6, 3, 7, 4, 8)
KROWS = TH + 16
WIN = 5
KEYS = WIN * TB
MODEL = 16384


def body(h, gain, wq, wk, wv, wo, seg, out, *s):
    (
        gath, wraw, kvraw, wcat, wov, gv, segs, part, kvp, zk, zkr, zq, zqr, sqp, kvw, att, cs, cr, own, es, er, el, xs, xr,
        in_sem, ga_s, ga_r, gc_r, w_s, w_r, zk_s, zk_r, zq_s, zq_r, k_s, k_r, kc_r, d_s, d_r, c_s, c_r, e_s, e_r, x_s, x_r,
    ) = s
    gx = lax.axis_index("gx")
    gy = lax.axis_index("gy")
    xlo, z = lax.div(gx, NZ), lax.rem(gx, NZ)
    xhi, y, core = lax.div(gy, 8), lax.rem(lax.div(gy, 2), 4), lax.rem(gy, 2)
    xot, hot, cot = 1 - xlo, 1 - xhi, 1 - core

    def zm(v):
        return lax.rem(v + NZ, NZ)

    def ym(v):
        return lax.rem(v + 4, 4)

    def at_z(d, xx=None):
        return {"gx": (xlo if xx is None else xx) * NZ + zm(z + d), "gy": gy}

    def at_y(yy):
        return {"gx": gx, "gy": xhi * 8 + yy * 2 + core}

    def blk(hh, yy, cc):
        return hh * 8 + yy * 2 + cc

    far = blk(hot, y, core)
    dev_x = {"gx": xot * NZ + z, "gy": gy}
    dev_h = {"gx": gx, "gy": far}
    dev_d = {"gx": xot * NZ + z, "gy": far}
    dev_c = {"gx": gx, "gy": blk(xhi, y, cot)}

    def rc(src, dst, ss, rs, dev):
        return pltpu.make_async_remote_copy(src_ref=src, dst_ref=dst, send_sem=ss, recv_sem=rs, device_id=dev, device_id_type=MESH)

    barrier = pltpu.get_barrier_semaphore()
    greet = [dev_x, dev_h, dev_d, dev_c] + [at_y(ym(y + d)) for d in (1, 2, 3)] + [at_z(d) for d in (1, 2, 3, 4, 5, -1, -2, -3, -4, -5)]
    for d in greet:
        pl.semaphore_signal(barrier, inc=1, device_id=d, device_id_type=MESH)
    is_core0 = core == 0
    head = pl.multiple_of((xhi * 4 + y) * HD, HD)
    mine = pl.ds(pl.multiple_of(xlo * TH, TH), TH)
    other = pl.ds(pl.multiple_of(xot * TH, TH), TH)
    loads = [
        pltpu.make_async_copy(h.at[mine], gath.at[gy, 0], in_sem.at[0]),
        pltpu.make_async_copy(wq, wraw.at[0], in_sem.at[1]),
        pltpu.make_async_copy(wo, wov.at[0], in_sem.at[2]),
        pltpu.make_async_copy(gain, gv.at[0], in_sem.at[3]),
        pltpu.make_async_copy(seg, segs, in_sem.at[4]),
    ]
    for c in loads:
        c.start()

    def kv_load(src):
        return pltpu.make_async_copy(src.at[:, pl.ds(head, HD)], kvraw.at[0], in_sem.at[5])

    def kv_send(src):
        return rc(src.at[:, pl.ds(head, HD)], kvraw.at[1], w_s.at[0], w_r.at[0], dev_x)

    @pl.when(is_core0)
    def _():
        kv_load(wk).start()

    @pl.when(core == 1)
    def _():
        kv_load(wv).start()

    pl.semaphore_wait(barrier, len(greet))

    def g_copy(dst, n, dev, src=None):
        return rc(dst if src is None else src, dst, ga_s, ga_r.at[n], dev)

    def gc_copy(ref):
        return rc(ref, ref, ga_s, gc_r, dev_c)

    ys = (2, 1, 3)
    at = {1: 4, 3: 1, 2: 7}
    by = {1: 1, 3: 4, 2: 7}
    g_copy(gath.at[gy, 1], 0, dev_x, h.at[other]).start()
    g_copy(gath.at[gy, 0], 10, dev_h, h.at[mine]).start()
    g_copy(gath.at[gy, 1], 11, dev_d, h.at[other]).start()
    for d in ys:
        g_copy(gath.at[gy, 0], at[d], at_y(ym(y + d)), h.at[mine]).start()

    cp_g = rc(gain, gv.at[1], w_s.at[1], w_r.at[1], dev_x)
    cp_q = [rc(wq.at[:, pl.ds(p * QW, QW)], wraw.at[1, :, pl.ds(p * QW, QW)], w_s.at[2 + p], w_r.at[2 + p], dev_x) for p in range(2)]
    cp_o = rc(wo, wov.at[1], w_s.at[4], w_r.at[4], dev_x)
    cp_g.start()
    rc(h.at[mine], gath.at[gy, 0], ga_s, gc_r, dev_c).start()

    for c in loads:
        c.wait()
    kv_load(wk).wait()

    def gain_column(f):
        return jnp.transpose(jnp.broadcast_to(gv[f], (HD, WIDTH)))

    def kv_weights(f):
        wcat[f, :, 0:HD] = (kvraw[f].astype(F32) * gain_column(f)).astype(BF)

    def q_weights(f, p):
        col = gain_column(f)
        for j in range(2 * p, 2 * p + 2):
            wcat[f, :, HD * (j + 1) : HD * (j + 2)] = (wraw[f, :, HD * j : HD * (j + 1)].astype(F32) * col).astype(BF)

    g_copy(gath.at[gy, 1], 0, dev_x).wait_recv()
    for d in ys:
        g_copy(gath.at[gy, 1], at[d] + 1, at_y(ym(y + d))).start()
    gc_copy(gath.at[gy, 1]).start()
    g_copy(gath.at[far, 0], 10, dev_h).wait_recv()
    g_copy(gath.at[far, 1], 11, dev_d).wait_recv()
    for d in ys:
        g_copy(gath.at[far], at[d] + 2, at_y(ym(y + d))).start()
    gc_copy(gath.at[far]).start()
    @pl.when(is_core0)
    def _():
        kv_send(wk).start()

    @pl.when(core == 1)
    def _():
        kv_send(wv).start()

    cp_q[0].start()
    kv_weights(0)
    for p in range(2):
        q_weights(0, p)

    def firsts(tq):
        start = jnp.zeros_like(tq)
        total = jnp.int32(0)
        for i in range(SEGS):
            start = jnp.where(tq >= total, total, start)
            total = total + segs[i]
        return start

    here = z * TB + xlo * TH
    lane = lax.broadcasted_iota(jnp.int32, (TH, HD), 1)
    tok = here + lax.broadcasted_iota(jnp.int32, (TH, HD), 0)
    pos = (tok - firsts(tok)).astype(F32)
    freq = jnp.exp((lax.rem(lane, HALF)).astype(F32) * (-2.0 / HD * math.log(ROPE_BASE)))
    angle = pos * freq
    cosine = jnp.cos(angle)
    sine = jnp.sin(angle)
    sine = jnp.where(lane < HALF, -sine, sine)

    def rotated(v):
        return v * cosine + pltpu.roll(v, HALF, 1) * sine

    for d in ys:
        b = blk(xhi, ym(y + d), core)
        g_copy(gath.at[b, 0], by[d], dev_c).wait_recv()
        g_copy(gath.at[b, 1], by[d] + 1, dev_c).wait_recv()
        gc_copy(gath.at[b]).start()
    rc(kvraw.at[0], kvraw.at[1], w_s.at[0], w_r.at[0], dev_x).wait_recv()
    cp_q[1].start()
    cp_g.wait_recv()
    kv_weights(1)
    for d in ys:
        b = blk(hot, ym(y + d), core)
        g_copy(gath.at[b], by[d] + 2, dev_c).wait_recv()
        gc_copy(gath.at[b]).start()
    gc_copy(gath.at[pl.ds(0, 8)]).wait_recv()

    ones = jnp.ones((8, WIDTH), BF)
    nt = (((1,), (1,)), ((), ()))

    def steps(jumps):
        ends = (*jumps, 1)
        runs = [(d, top, end) for d in range(2) for top, end in zip((8 - d, *(j - 1 for j in jumps)), ends)]
        runs.sort(key=lambda r: -r[1])
        most = max(top - end for _, top, end in runs) + 1
        return [[(d, top - t) for d, top, end in runs if top - t >= end] for t in range(most)]

    def target(d, n):
        return zm(z + (1 - 2 * d) * n)

    def leg(d, n, jumps):
        return at_z((1 - 2 * d) * (n if n in jumps else 1))

    def k_ring(d, n):
        return rc(zk.at[d, n], zkr.at[d, n], zk_s.at[d], zk_r.at[d, n], leg(d, n, JK))

    def q_ring(p):
        return lambda d, n: rc(zq.at[p, d, n], zqr.at[p, d, n], zq_s.at[p, d], zq_r.at[p, d, n], leg(d, n, JQ))

    def before(d, n, jumps):
        return n + 1 <= 8 - d and n + 1 not in jumps

    def read_kv(d, n):
        k_ring(d, n).wait_recv()
        v = zkr[d, n].astype(F32)
        return v[0:TH], v[TH : TH + 8] + v[TH + 8 :]

    def total(jumps, mine, ring, got):
        t = mine
        for d in range(2):
            for n in (1, *jumps):
                ring(d, n).wait_recv()
                t = t + got[d, n].astype(F32)
        return t

    def rows_of(pairs, f):
        return jnp.concatenate([gath[target(d, n), f] for d, n in pairs], axis=0)

    def q_product(p, pairs):
        cols = slice(HD + p * QW, HD + p * QW + QW)
        res = sum(jnp.dot(rows_of(pairs, f), wcat[f, :, cols], preferred_element_type=F32) for f in range(2))
        for i, (d, n) in enumerate(pairs):
            part[p, d, n] = res[i * TH : i * TH + TH]

    def sq_product(pairs):
        r = jnp.zeros((8, len(pairs) * TH), F32)
        for f in range(2):
            xf = rows_of(pairs, f).astype(F32)
            r = r + lax.dot_general(ones, (xf * xf).astype(BF), nt, preferred_element_type=F32)
        for i, (d, n) in enumerate(pairs):
            m = i // 2 * TB
            t = r[:, m : m + TB]
            sqp[d, n] = pltpu.roll(t, TH, 1) if i % 2 else t

    def k_step(pairs):
        for d, n in pairs:
            t, q = kvp[d, n], sqp[d, n]
            if before(d, n, JK):
                t2, q2 = read_kv(d, n + 1)
                t, q = t + t2, q + q2
            hi = q.astype(BF).astype(F32)
            zk[d, n] = jnp.concatenate([t, hi, q - hi], axis=0).astype(BF)
            k_ring(d, n).start()

    def q_step(p, pairs):
        for d, n in pairs:
            t = part[p, d, n]
            if before(d, n, JQ):
                q_ring(p)(d, n + 1).wait_recv()
                t = t + zqr[p, d, n + 1].astype(F32)
            zq[p, d, n] = t.astype(BF)
            q_ring(p)(d, n).start()

    me = (0, 0)
    k_steps, q_steps = steps(JK), steps(JQ)
    def kv_product(pairs):
        res = sum(jnp.dot(rows_of(pairs, f), wcat[f, :, 0:HD], preferred_element_type=F32) for f in range(2))
        for i, (d, n) in enumerate(pairs):
            kvp[d, n] = res[i * TH : i * TH + TH]

    kv_product(k_steps[0])
    sq_product(k_steps[0])
    k_step(k_steps[0])
    def k_copy(d, xx, n, dev, dd=None):
        to = d if dd is None else dd
        return rc(kvw.at[core, d, xx], kvw.at[core, to, xx], k_s, k_r.at[to, n], dev)

    def kc_copy(d, xx):
        return rc(kvw.at[core, d, xx], kvw.at[core, d, xx], k_s, kc_r, dev_c)

    def window_sends():
        kv, squares = kvp[me], sqp[me]
        for d in range(2):
            for n in (1, *JK):
                t, q = read_kv(d, n)
                kv, squares = kv + t, squares + q
        squares = jnp.transpose(jnp.broadcast_to(squares[0:1], (HD, TB)))[0:TH]
        scale = lax.rsqrt(squares / MODEL + EPS)
        kv = kv * scale
        kvw[core, 0, xlo] = jnp.where(is_core0, rotated(kv), kv).astype(BF)
        for d in range(WIN - 1, 0, -1):
            k_copy(0, xlo, 0, at_z(d), d).start()
        k_copy(0, xlo, 1, dev_x).start()
        kc_copy(0, xlo).start()
        return scale

    def queries_of(p):
        t = total(JQ, part[(p, *me)], q_ring(p), zqr.at[p])
        return [rotated(t[:, HD * j : HD * (j + 1)] * scale).astype(BF) for j in range(2)]

    lag = 2
    n_q = len(q_steps)
    for t in range(n_q + lag):
        if t == 0:
            cp_q[0].wait_recv()
            q_weights(1, 0)
        if t == lag:
            cp_q[1].wait_recv()
            cp_o.start()
            q_weights(1, 1)
        now = [(p, t - p * lag) for p in range(2) if 0 <= t - p * lag < n_q]
        for p, i in now:
            q_product(p, q_steps[i] + [me] * (i == n_q - 1))
        if 0 < t < len(k_steps):
            pairs = k_steps[t] + [me] * (t == len(k_steps) - 1)
            kv_product(pairs)
            sq_product(pairs)
            k_step(k_steps[t])
        for p, i in now:
            q_step(p, q_steps[i])
        if t == len(k_steps):
            scale = window_sends()

    queries = queries_of(0)
    k_copy(0, xot, 1, dev_x).wait_recv()
    kc_copy(0, xot).start()
    for d in range(1, WIN):
        k_copy(d, xlo, 0, dev_x).wait_recv()
        k_copy(d, xlo, 1, dev_x).start()
        kc_copy(d, xlo).start()
    for d in range(1, WIN):
        k_copy(d, xot, 1, dev_x).wait_recv()
        kc_copy(d, xot).start()
    queries = jnp.concatenate(queries + queries_of(1), axis=0)
    rc(kvw.at[cot], kvw.at[cot], k_s, kc_r, dev_c).wait_recv()

    keys = kvw[0].reshape(KEYS, HD)
    values = kvw[1].reshape(KEYS, HD)
    scores = lax.dot_general(queries, keys, nt, preferred_element_type=F32) * (1.0 / math.sqrt(HD))
    n = lax.broadcasted_iota(jnp.int32, (TH, KEYS), 1)
    tk = z * TB + n - 2 * TB * lax.div(n, TB)
    tq = here + lax.broadcasted_iota(jnp.int32, (TH, KEYS), 0)
    allowed = (tk >= firsts(tq)) & (tk <= tq)

    def d_copy(d, b, p, hops=1):
        return rc(att.at[b, p], att.at[b, p], d_s.at[d], d_r.at[b, p], at_z((1 - 2 * d) * hops))

    for j in range(4):
        sc = jnp.where(allowed, scores[TH * j : TH * (j + 1)], -1e30)
        e = jnp.exp(sc - jnp.max(sc, axis=1, keepdims=True))
        e = jnp.where(allowed, e, 0.0)
        o = jnp.dot(e.astype(BF), values, preferred_element_type=F32) / jnp.sum(e, axis=1, keepdims=True)
        att[z, j // 2, :, HD * (j % 2) : HD * (j % 2 + 1)] = o.astype(BF)
        if j % 2:
            for d in range(2):
                for hops in JD:
                    d_copy(d, z, j // 2, hops).start()
                d_copy(d, z, j // 2).start()
    cp_o.wait_recv()

    def pass_on(d, n):
        b = zm(z - (1 - 2 * d) * n)
        for p in range(2):
            d_copy(d, b, p).wait_recv()
            if n + 1 not in JD and n < 8 - d:
                d_copy(d, b, p).start()

    def c_copy(b):
        m = lax.div(b, 2)
        return rc(cs.at[m], cr.at[m], c_s, c_r.at[m], dev_c)

    def e_copy(b, yy):
        hh, m = lax.div(b, 8), lax.div(b, 2)
        return rc(es.at[m], er.at[hh, y], e_s, e_r.at[hh, y], at_y(yy))

    def out_product(blocks):
        halves = [jnp.concatenate([att[b, p] for b in blocks], axis=0) for p in range(2)]
        for g in range(2):
            t = sum(jnp.dot(halves[p], wov[g, p * QW : p * QW + QW], preferred_element_type=F32) for p in range(2))
            cols = slice(g * WIDTH, g * WIDTH + WIDTH)
            same = lax.rem(blocks[0], 2) == core

            @pl.when(same)
            def _():
                for i, b in enumerate(blocks):
                    own[lax.div(b, 2), :, cols] = t[i * TH : i * TH + TH]

            @pl.when(jnp.logical_not(same))
            def _():
                for i, b in enumerate(blocks):
                    cs[lax.div(b, 2), :, cols] = t[i * TH : i * TH + TH].astype(BF)

        @pl.when(lax.rem(blocks[0], 2) != core)
        def _():
            for b in blocks:
                c_copy(b).start()

    def out_send(b):
        @pl.when(lax.rem(b, 2) == core)
        def _():
            m = lax.div(b, 2)
            c_copy(b).wait_recv()
            t = own[m] + cr[m].astype(F32)
            yb = lax.rem(m, 4)

            @pl.when(yb == y)
            def _():
                el[lax.div(b, 8)] = t

            @pl.when(yb != y)
            def _():
                es[m] = t.astype(BF)
                e_copy(b, yb).start()

    def both(n):
        return [zm(z - n), zm(z + n)][: 1 if n in (0, 8) else 2]

    done = (0, *ORDER)
    for i in range(1, 11):
        if i < 9:
            for d in range(2 if done[i] < 8 else 1):
                pass_on(d, done[i])
        if 1 < i < 9:
            for b in both(done[i - 2]):
                out_send(b)
        if i < 10:
            out_product(both(done[i - 1]))
        if i > 8:
            for b in both(done[i - 2]):
                out_send(b)

    def y_sum(hh):
        t = el[hh]
        for d in ys:
            yy = ym(y + d)
            rc(es.at[0], er.at[hh, yy], e_s, e_r.at[hh, yy], at_y(yy)).wait_recv()
            t = t + er[hh, yy].astype(F32)
        return t

    def x_copy(n, dev):
        return rc(xs.at[n], xr.at[n], x_s, x_r.at[n], dev)

    away = y_sum(hot)
    xs[0] = away[:, 0:WIDTH].astype(BF)
    x_copy(0, dev_h).start()
    xs[1] = away[:, WIDTH:].astype(BF)
    x_copy(1, dev_d).start()
    home = y_sum(xhi)
    xs[2] = home[:, WIDTH:].astype(BF)
    x_copy(2, dev_x).start()
    x_copy(0, dev_h).wait_recv()
    out[mine, :] = (home[:, 0:WIDTH] + xr[0].astype(F32)).astype(BF)
    x_copy(1, dev_d).wait_recv()
    x_copy(2, dev_x).wait_recv()
    out[other, :] = (xr[1].astype(F32) + xr[2].astype(F32)).astype(BF)

    def left(ref, sem):
        rc(ref, ref, sem, x_r.at[0], dev_x).wait_send()

    pieces = gath.reshape(2 * NZ, TH, WIDTH)
    left(pieces.at[pl.ds(0, 31)], ga_s)
    left(kvraw.at[0], w_s.at[0])
    cp_g.wait_send()
    for c in cp_q:
        c.wait_send()
    cp_o.wait_send()
    for d in range(2):
        left(zk.at[d, pl.ds(0, 8 - d)], zk_s.at[d])
        for p in range(2):
            left(zq.at[p, d, pl.ds(0, 8 - d)], zq_s.at[p, d])
        left(att.at[pl.ds(0, 8 - d)], d_s.at[d])
    left(kvw.reshape(4 * WIN, TH, HD).at[pl.ds(0, 4 * WIN - 1)], k_s)
    left(cs, c_s)
    left(es.at[pl.ds(0, 6)], e_s)
    left(xs, x_s)


def shards(hidden_in, norm_gain, w_query, w_key, w_value, w_out, seg_lengths):
    v = pltpu.VMEM
    dma = pltpu.SemaphoreType.DMA
    scratch = [
        v((NZ, 2, TH, WIDTH), BF),
        v((2, WIDTH, WIDTH), BF),
        v((2, WIDTH, HD), BF),
        v((2, WIDTH, COLS), BF),
        v((2, WIDTH, WIDTH), BF),
        v((2, 1, WIDTH), F32),
        pltpu.SMEM((SEGS,), jnp.int32),
        v((2, 2, 9, TH, QW), F32),
        v((2, 9, TH, HD), F32),
        v((2, 9, KROWS, HD), BF),
        v((2, 9, KROWS, HD), BF),
        v((2, 2, 9, TH, QW), BF),
        v((2, 2, 9, TH, QW), BF),
        v((2, 9, 8, TB), F32),
        v((2, WIN, 2, TH, HD), BF),
        v((NZ, 2, TH, QW), BF),
        v((8, TH, 2 * WIDTH), BF),
        v((8, TH, 2 * WIDTH), BF),
        v((8, TH, 2 * WIDTH), F32),
        v((8, TH, 2 * WIDTH), BF),
        v((2, 4, TH, 2 * WIDTH), BF),
        v((2, TH, 2 * WIDTH), F32),
        v((3, TH, WIDTH), BF),
        v((3, TH, WIDTH), BF),
        dma((6,)),
        dma, dma((12,)), dma,
        dma((5,)), dma((5,)),
        dma((2,)), dma((2, 9)),
        dma((2, 2)), dma((2, 2, 9)),
        dma, dma((WIN, 2)), dma,
        dma((2,)), dma((NZ, 2)),
        dma, dma((8,)),
        dma, dma((2, 4)),
        dma, dma((3,)),
    ]
    anywhere = pl.BlockSpec(memory_space=pl.ANY)
    return pl.pallas_call(
        body,
        name="attention_block",
        out_shape=jax.ShapeDtypeStruct((TB, WIDTH), BF),
        in_specs=[anywhere] * 7,
        out_specs=pl.BlockSpec(memory_space=pltpu.VMEM),
        scratch_shapes=scratch,
        compiler_params=pltpu.CompilerParams(collective_id=0, has_side_effects=True, vmem_limit_bytes=62 * 2**20),
        cost_estimate=pl.CostEstimate(flops=3 * 10**9, bytes_accessed=3 * 10**6, transcendentals=10**6),
    )(hidden_in, norm_gain.reshape(1, WIDTH), w_query, w_key, w_value, w_out, seg_lengths)


def solution(mesh):
    in_specs = (P("gy", "gx"), P("gx"), P("gx", "gy"), P("gx", None), P("gx", None), P("gy", "gx"), P())
    return jax.shard_map(shards, mesh=mesh, in_specs=in_specs, out_specs=P("gy", "gx"), check_vma=False)
```

```python
import math

import jax
import jax.numpy as jnp
from jax import lax
from jax.experimental import pallas as pl
from jax.experimental.pallas import tpu as pltpu
from jax.sharding import PartitionSpec as P

MESH = pl.DeviceIdType.MESH
HD = 128
HALF = HD // 2
SEGS = 8
ROPE_BASE = 500000.0
EPS = 1e-05
BF = jnp.bfloat16
F32 = jnp.float32

NZ = 16
TB = 128
TH = 64
WIDTH = 512
QW = 256
COLS = HD + WIDTH
JK = (5,)
JQ = (4,)
JD = (5,)
ORDER = (1, 5, 2, 6, 3, 7, 4, 8)
KROWS = TH + 16
WIN = 5
KEYS = WIN * TB
MODEL = 16384


def body(h, gain, wq, wk, wv, wo, seg, out, *s):
    (
        gath, wraw, kvraw, wcat, wov, gv, segs, part, kvp, zk, zkr, zq, zqr, sqp, kvw, att, cs, cr, own, es, er, el, xs, xr,
        in_sem, ga_s, ga_r, gc_r, w_s, w_r, zk_s, zk_r, zq_s, zq_r, k_s, k_r, kc_r, d_s, d_r, c_s, c_r, e_s, e_r, x_s, x_r,
    ) = s
    gx = lax.axis_index("gx")
    gy = lax.axis_index("gy")
    xlo, z = lax.div(gx, NZ), lax.rem(gx, NZ)
    xhi, y, core = lax.div(gy, 8), lax.rem(lax.div(gy, 2), 4), lax.rem(gy, 2)
    xot, hot, cot = 1 - xlo, 1 - xhi, 1 - core

    def zm(v):
        return lax.rem(v + NZ, NZ)

    def ym(v):
        return lax.rem(v + 4, 4)

    def at_z(d, xx=None):
        return {"gx": (xlo if xx is None else xx) * NZ + zm(z + d), "gy": gy}

    def at_y(yy):
        return {"gx": gx, "gy": xhi * 8 + yy * 2 + core}

    def blk(hh, yy, cc):
        return hh * 8 + yy * 2 + cc

    far = blk(hot, y, core)
    dev_x = {"gx": xot * NZ + z, "gy": gy}
    dev_h = {"gx": gx, "gy": far}
    dev_d = {"gx": xot * NZ + z, "gy": far}
    dev_c = {"gx": gx, "gy": blk(xhi, y, cot)}

    def rc(src, dst, ss, rs, dev):
        return pltpu.make_async_remote_copy(src_ref=src, dst_ref=dst, send_sem=ss, recv_sem=rs, device_id=dev, device_id_type=MESH)

    barrier = pltpu.get_barrier_semaphore()
    greet = [dev_x, dev_h, dev_d, dev_c] + [at_y(ym(y + d)) for d in (1, 2, 3)] + [at_z(d) for d in (1, 2, 3, 4, 5, -1, -2, -3, -4, -5)]
    for d in greet:
        pl.semaphore_signal(barrier, inc=1, device_id=d, device_id_type=MESH)
    is_core0 = core == 0
    head = pl.multiple_of((xhi * 4 + y) * HD, HD)
    mine = pl.ds(pl.multiple_of(xlo * TH, TH), TH)
    other = pl.ds(pl.multiple_of(xot * TH, TH), TH)
    loads = [
        pltpu.make_async_copy(h.at[mine], gath.at[gy, 0], in_sem.at[0]),
        pltpu.make_async_copy(wq, wraw.at[0], in_sem.at[1]),
        pltpu.make_async_copy(wo, wov.at[0], in_sem.at[2]),
        pltpu.make_async_copy(gain, gv.at[0], in_sem.at[3]),
        pltpu.make_async_copy(seg, segs, in_sem.at[4]),
    ]
    for c in loads:
        c.start()

    def kv_load(src):
        return pltpu.make_async_copy(src.at[:, pl.ds(head, HD)], kvraw.at[0], in_sem.at[5])

    def kv_send(src):
        return rc(src.at[:, pl.ds(head, HD)], kvraw.at[1], w_s.at[0], w_r.at[0], dev_x)

    @pl.when(is_core0)
    def _():
        kv_load(wk).start()

    @pl.when(core == 1)
    def _():
        kv_load(wv).start()

    pl.semaphore_wait(barrier, len(greet))

    def g_copy(dst, n, dev, src=None):
        return rc(dst if src is None else src, dst, ga_s, ga_r.at[n], dev)

    def gc_copy(ref):
        return rc(ref, ref, ga_s, gc_r, dev_c)

    ys = (2, 1, 3)
    at = {1: 4, 3: 1, 2: 7}
    at2 = {1: 13, 3: 12, 2: 14}
    by2 = {1: 12, 3: 13, 2: 14}
    by = {1: 1, 3: 4, 2: 7}
    g_copy(gath.at[gy, 1], 0, dev_x, h.at[other]).start()
    g_copy(gath.at[gy, 0], 10, dev_h, h.at[mine]).start()
    g_copy(gath.at[gy, 1], 11, dev_d, h.at[other]).start()
    for d in ys:
        g_copy(gath.at[gy, 0], at[d], at_y(ym(y + d)), h.at[mine]).start()

    cp_g = rc(gain, gv.at[1], w_s.at[1], w_r.at[1], dev_x)
    cp_q = [rc(wq.at[:, pl.ds(p * QW, QW)], wraw.at[1, :, pl.ds(p * QW, QW)], w_s.at[2 + p], w_r.at[2 + p], dev_x) for p in range(2)]
    cp_o = rc(wo, wov.at[1], w_s.at[4], w_r.at[4], dev_x)
    cp_g.start()
    rc(h.at[mine], gath.at[gy, 0], ga_s, gc_r, dev_c).start()

    for c in loads:
        c.wait()
    kv_load(wk).wait()

    def gain_column(f):
        return jnp.transpose(jnp.broadcast_to(gv[f], (HD, WIDTH)))

    def kv_weights(f):
        wcat[f, :, 0:HD] = (kvraw[f].astype(F32) * gain_column(f)).astype(BF)

    def q_weights(f, p):
        col = gain_column(f)
        for j in range(2 * p, 2 * p + 2):
            wcat[f, :, HD * (j + 1) : HD * (j + 2)] = (wraw[f, :, HD * j : HD * (j + 1)].astype(F32) * col).astype(BF)

    g_copy(gath.at[far, 1], 11, dev_d).wait_recv()
    for d in ys:
        g_copy(gath.at[far, 1], at2[d], at_y(ym(y + d))).start()
    gc_copy(gath.at[far, 1]).start()
    g_copy(gath.at[gy, 1], 0, dev_x).wait_recv()
    for d in ys:
        g_copy(gath.at[gy, 1], at[d] + 1, at_y(ym(y + d))).start()
    gc_copy(gath.at[gy, 1]).start()
    g_copy(gath.at[far, 0], 10, dev_h).wait_recv()
    for d in ys:
        g_copy(gath.at[far, 0], at[d] + 2, at_y(ym(y + d))).start()
    gc_copy(gath.at[far, 0]).start()
    @pl.when(is_core0)
    def _():
        kv_send(wk).start()

    @pl.when(core == 1)
    def _():
        kv_send(wv).start()

    for c in cp_q:
        c.start()
    kv_weights(0)
    for p in range(2):
        q_weights(0, p)

    def firsts(tq):
        start = jnp.zeros_like(tq)
        total = jnp.int32(0)
        for i in range(SEGS):
            start = jnp.where(tq >= total, total, start)
            total = total + segs[i]
        return start

    here = z * TB + xlo * TH
    lane = lax.broadcasted_iota(jnp.int32, (TH, HD), 1)
    tok = here + lax.broadcasted_iota(jnp.int32, (TH, HD), 0)
    pos = (tok - firsts(tok)).astype(F32)
    freq = jnp.exp((lax.rem(lane, HALF)).astype(F32) * (-2.0 / HD * math.log(ROPE_BASE)))
    angle = pos * freq
    cosine = jnp.cos(angle)
    sine = jnp.sin(angle)
    sine = jnp.where(lane < HALF, -sine, sine)

    def rotated(v):
        return v * cosine + pltpu.roll(v, HALF, 1) * sine

    for d in ys:
        b = blk(xhi, ym(y + d), core)
        g_copy(gath.at[b, 0], by[d], dev_c).wait_recv()
        g_copy(gath.at[b, 1], by[d] + 1, dev_c).wait_recv()
        gc_copy(gath.at[b]).start()
    for d in ys:
        b = blk(hot, ym(y + d), core)
        g_copy(gath.at[b, 1], by2[d], dev_c).wait_recv()
        g_copy(gath.at[b, 0], by[d] + 2, dev_c).wait_recv()
        gc_copy(gath.at[b]).start()
    rc(kvraw.at[0], kvraw.at[1], w_s.at[0], w_r.at[0], dev_x).wait_recv()
    cp_g.wait_recv()
    kv_weights(1)
    gc_copy(gath.at[pl.ds(0, 8)]).wait_recv()

    ones = jnp.ones((8, WIDTH), BF)
    nt = (((1,), (1,)), ((), ()))

    def steps(jumps):
        ends = (*jumps, 1)
        runs = [(d, top, end) for d in range(2) for top, end in zip((8 - d, *(j - 1 for j in jumps)), ends)]
        runs.sort(key=lambda r: -r[1])
        most = max(top - end for _, top, end in runs) + 1
        return [[(d, top - t) for d, top, end in runs if top - t >= end] for t in range(most)]

    def target(d, n):
        return zm(z + (1 - 2 * d) * n)

    def leg(d, n, jumps):
        return at_z((1 - 2 * d) * (n if n in jumps else 1))

    def k_ring(d, n):
        return rc(zk.at[d, n], zkr.at[d, n], zk_s.at[d], zk_r.at[d, n], leg(d, n, JK))

    def q_ring(p):
        return lambda d, n: rc(zq.at[p, d, n], zqr.at[p, d, n], zq_s.at[p, d], zq_r.at[p, d, n], leg(d, n, JQ))

    def before(d, n, jumps):
        return n + 1 <= 8 - d and n + 1 not in jumps

    def read_kv(d, n):
        k_ring(d, n).wait_recv()
        v = zkr[d, n].astype(F32)
        return v[0:TH], v[TH : TH + 8] + v[TH + 8 :]

    def total(jumps, mine, ring, got):
        t = mine
        for d in range(2):
            for n in (1, *jumps):
                ring(d, n).wait_recv()
                t = t + got[d, n].astype(F32)
        return t

    def rows_of(pairs, f):
        return jnp.concatenate([gath[target(d, n), f] for d, n in pairs], axis=0)

    def q_product(p, pairs):
        cols = slice(HD + p * QW, HD + p * QW + QW)
        res = sum(jnp.dot(rows_of(pairs, f), wcat[f, :, cols], preferred_element_type=F32) for f in range(2))
        for i, (d, n) in enumerate(pairs):
            part[p, d, n] = res[i * TH : i * TH + TH]

    def sq_product(pairs):
        r = jnp.zeros((8, len(pairs) * TH), F32)
        for f in range(2):
            xf = rows_of(pairs, f).astype(F32)
            r = r + lax.dot_general(ones, (xf * xf).astype(BF), nt, preferred_element_type=F32)
        for i, (d, n) in enumerate(pairs):
            m = i // 2 * TB
            t = r[:, m : m + TB]
            sqp[d, n] = pltpu.roll(t, TH, 1) if i % 2 else t

    def k_step(pairs):
        for d, n in pairs:
            t, q = kvp[d, n], sqp[d, n]
            if before(d, n, JK):
                t2, q2 = read_kv(d, n + 1)
                t, q = t + t2, q + q2
            hi = q.astype(BF).astype(F32)
            zk[d, n] = jnp.concatenate([t, hi, q - hi], axis=0).astype(BF)
            k_ring(d, n).start()

    def q_step(p, pairs):
        for d, n in pairs:
            t = part[p, d, n]
            if before(d, n, JQ):
                q_ring(p)(d, n + 1).wait_recv()
                t = t + zqr[p, d, n + 1].astype(F32)
            zq[p, d, n] = t.astype(BF)
            q_ring(p)(d, n).start()

    me = (0, 0)
    k_steps, q_steps = steps(JK), steps(JQ)
    def kv_product(pairs):
        res = sum(jnp.dot(rows_of(pairs, f), wcat[f, :, 0:HD], preferred_element_type=F32) for f in range(2))
        for i, (d, n) in enumerate(pairs):
            kvp[d, n] = res[i * TH : i * TH + TH]

    kv_product(k_steps[0])
    sq_product(k_steps[0])
    k_step(k_steps[0])
    def k_copy(d, xx, n, dev, dd=None):
        to = d if dd is None else dd
        return rc(kvw.at[core, d, xx], kvw.at[core, to, xx], k_s, k_r.at[to, n], dev)

    def kc_copy(d, xx):
        return rc(kvw.at[core, d, xx], kvw.at[core, d, xx], k_s, kc_r, dev_c)

    def window_sends():
        kv, squares = kvp[me], sqp[me]
        for d in range(2):
            for n in (1, *JK):
                t, q = read_kv(d, n)
                kv, squares = kv + t, squares + q
        squares = jnp.transpose(jnp.broadcast_to(squares[0:1], (HD, TB)))[0:TH]
        scale = lax.rsqrt(squares / MODEL + EPS)
        kv = kv * scale
        kvw[core, 0, xlo] = jnp.where(is_core0, rotated(kv), kv).astype(BF)
        for d in range(WIN - 1, 0, -1):
            k_copy(0, xlo, 0, at_z(d), d).start()
        k_copy(0, xlo, 1, dev_x).start()
        kc_copy(0, xlo).start()
        return scale

    def queries_of(p):
        t = total(JQ, part[(p, *me)], q_ring(p), zqr.at[p])
        return [rotated(t[:, HD * j : HD * (j + 1)] * scale).astype(BF) for j in range(2)]

    lag = 2
    n_q = len(q_steps)
    for t in range(n_q + lag):
        if t == 0:
            cp_q[0].wait_recv()
            q_weights(1, 0)
        if t == lag:
            cp_q[1].wait_recv()
            cp_o.start()
            q_weights(1, 1)
        now = [(p, t - p * lag) for p in range(2) if 0 <= t - p * lag < n_q]
        for p, i in now:
            q_product(p, q_steps[i] + [me] * (i == n_q - 1))
        if 0 < t < len(k_steps):
            pairs = k_steps[t] + [me] * (t == len(k_steps) - 1)
            kv_product(pairs)
            sq_product(pairs)
            k_step(k_steps[t])
        for p, i in now:
            q_step(p, q_steps[i])
        if t == len(k_steps):
            scale = window_sends()

    queries = queries_of(0)
    k_copy(0, xot, 1, dev_x).wait_recv()
    kc_copy(0, xot).start()
    for d in range(1, WIN):
        k_copy(d, xlo, 0, dev_x).wait_recv()
        k_copy(d, xlo, 1, dev_x).start()
        kc_copy(d, xlo).start()
    for d in range(1, WIN):
        k_copy(d, xot, 1, dev_x).wait_recv()
        kc_copy(d, xot).start()
    queries = jnp.concatenate(queries + queries_of(1), axis=0)
    rc(kvw.at[cot], kvw.at[cot], k_s, kc_r, dev_c).wait_recv()

    keys = kvw[0].reshape(KEYS, HD)
    values = kvw[1].reshape(KEYS, HD)
    scores = lax.dot_general(queries, keys, nt, preferred_element_type=F32) * (1.0 / math.sqrt(HD))
    n = lax.broadcasted_iota(jnp.int32, (TH, KEYS), 1)
    tk = z * TB + n - 2 * TB * lax.div(n, TB)
    tq = here + lax.broadcasted_iota(jnp.int32, (TH, KEYS), 0)
    allowed = (tk >= firsts(tq)) & (tk <= tq)

    def d_copy(d, b, p, hops=1):
        return rc(att.at[b, p], att.at[b, p], d_s.at[d], d_r.at[b, p], at_z((1 - 2 * d) * hops))

    for j in range(4):
        sc = jnp.where(allowed, scores[TH * j : TH * (j + 1)], -1e30)
        e = jnp.exp(sc - jnp.max(sc, axis=1, keepdims=True))
        e = jnp.where(allowed, e, 0.0)
        o = jnp.dot(e.astype(BF), values, preferred_element_type=F32) / jnp.sum(e, axis=1, keepdims=True)
        att[z, j // 2, :, HD * (j % 2) : HD * (j % 2 + 1)] = o.astype(BF)
        if j % 2:
            for d in range(2):
                for hops in JD:
                    d_copy(d, z, j // 2, hops).start()
                d_copy(d, z, j // 2).start()
    cp_o.wait_recv()

    def pass_on(d, n):
        b = zm(z - (1 - 2 * d) * n)
        for p in range(2):
            d_copy(d, b, p).wait_recv()
            if n + 1 not in JD and n < 8 - d:
                d_copy(d, b, p).start()

    def c_copy(b):
        m = lax.div(b, 2)
        return rc(cs.at[m], cr.at[m], c_s, c_r.at[m], dev_c)

    def e_copy(b, yy):
        hh, m = lax.div(b, 8), lax.div(b, 2)
        return rc(es.at[m], er.at[hh, y], e_s, e_r.at[hh, y], at_y(yy))

    def out_product(blocks):
        halves = [jnp.concatenate([att[b, p] for b in blocks], axis=0) for p in range(2)]
        for g in range(2):
            t = sum(jnp.dot(halves[p], wov[g, p * QW : p * QW + QW], preferred_element_type=F32) for p in range(2))
            cols = slice(g * WIDTH, g * WIDTH + WIDTH)
            same = lax.rem(blocks[0], 2) == core

            @pl.when(same)
            def _():
                for i, b in enumerate(blocks):
                    own[lax.div(b, 2), :, cols] = t[i * TH : i * TH + TH]

            @pl.when(jnp.logical_not(same))
            def _():
                for i, b in enumerate(blocks):
                    cs[lax.div(b, 2), :, cols] = t[i * TH : i * TH + TH].astype(BF)

        @pl.when(lax.rem(blocks[0], 2) != core)
        def _():
            for b in blocks:
                c_copy(b).start()

    def out_send(b):
        @pl.when(lax.rem(b, 2) == core)
        def _():
            m = lax.div(b, 2)
            c_copy(b).wait_recv()
            t = own[m] + cr[m].astype(F32)
            yb = lax.rem(m, 4)

            @pl.when(yb == y)
            def _():
                el[lax.div(b, 8)] = t

            @pl.when(yb != y)
            def _():
                es[m] = t.astype(BF)
                e_copy(b, yb).start()

    def both(n):
        return [zm(z - n), zm(z + n)][: 1 if n in (0, 8) else 2]

    done = (0, *ORDER)
    for i in range(1, 11):
        if i < 9:
            for d in range(2 if done[i] < 8 else 1):
                pass_on(d, done[i])
        if 1 < i < 9:
            for b in both(done[i - 2]):
                out_send(b)
        if i < 10:
            out_product(both(done[i - 1]))
        if i > 8:
            for b in both(done[i - 2]):
                out_send(b)

    def y_sum(hh):
        t = el[hh]
        for d in ys:
            yy = ym(y + d)
            rc(es.at[0], er.at[hh, yy], e_s, e_r.at[hh, yy], at_y(yy)).wait_recv()
            t = t + er[hh, yy].astype(F32)
        return t

    def x_copy(n, dev):
        return rc(xs.at[n], xr.at[n], x_s, x_r.at[n], dev)

    away = y_sum(hot)
    xs[0] = away[:, 0:WIDTH].astype(BF)
    x_copy(0, dev_h).start()
    xs[1] = away[:, WIDTH:].astype(BF)
    x_copy(1, dev_d).start()
    home = y_sum(xhi)
    xs[2] = home[:, WIDTH:].astype(BF)
    x_copy(2, dev_x).start()
    x_copy(0, dev_h).wait_recv()
    out[mine, :] = (home[:, 0:WIDTH] + xr[0].astype(F32)).astype(BF)
    x_copy(1, dev_d).wait_recv()
    x_copy(2, dev_x).wait_recv()
    out[other, :] = (xr[1].astype(F32) + xr[2].astype(F32)).astype(BF)

    def left(ref, sem):
        rc(ref, ref, sem, x_r.at[0], dev_x).wait_send()

    pieces = gath.reshape(2 * NZ, TH, WIDTH)
    left(pieces.at[pl.ds(0, 31)], ga_s)
    left(kvraw.at[0], w_s.at[0])
    cp_g.wait_send()
    for c in cp_q:
        c.wait_send()
    cp_o.wait_send()
    for d in range(2):
        left(zk.at[d, pl.ds(0, 8 - d)], zk_s.at[d])
        for p in range(2):
            left(zq.at[p, d, pl.ds(0, 8 - d)], zq_s.at[p, d])
        left(att.at[pl.ds(0, 8 - d)], d_s.at[d])
    left(kvw.reshape(4 * WIN, TH, HD).at[pl.ds(0, 4 * WIN - 1)], k_s)
    left(cs, c_s)
    left(es.at[pl.ds(0, 6)], e_s)
    left(xs, x_s)


def shards(hidden_in, norm_gain, w_query, w_key, w_value, w_out, seg_lengths):
    v = pltpu.VMEM
    dma = pltpu.SemaphoreType.DMA
    scratch = [
        v((NZ, 2, TH, WIDTH), BF),
        v((2, WIDTH, WIDTH), BF),
        v((2, WIDTH, HD), BF),
        v((2, WIDTH, COLS), BF),
        v((2, WIDTH, WIDTH), BF),
        v((2, 1, WIDTH), F32),
        pltpu.SMEM((SEGS,), jnp.int32),
        v((2, 2, 9, TH, QW), F32),
        v((2, 9, TH, HD), F32),
        v((2, 9, KROWS, HD), BF),
        v((2, 9, KROWS, HD), BF),
        v((2, 2, 9, TH, QW), BF),
        v((2, 2, 9, TH, QW), BF),
        v((2, 9, 8, TB), F32),
        v((2, WIN, 2, TH, HD), BF),
        v((NZ, 2, TH, QW), BF),
        v((8, TH, 2 * WIDTH), BF),
        v((8, TH, 2 * WIDTH), BF),
        v((8, TH, 2 * WIDTH), F32),
        v((8, TH, 2 * WIDTH), BF),
        v((2, 4, TH, 2 * WIDTH), BF),
        v((2, TH, 2 * WIDTH), F32),
        v((3, TH, WIDTH), BF),
        v((3, TH, WIDTH), BF),
        dma((6,)),
        dma, dma((15,)), dma,
        dma((5,)), dma((5,)),
        dma((2,)), dma((2, 9)),
        dma((2, 2)), dma((2, 2, 9)),
        dma, dma((WIN, 2)), dma,
        dma((2,)), dma((NZ, 2)),
        dma, dma((8,)),
        dma, dma((2, 4)),
        dma, dma((3,)),
    ]
    anywhere = pl.BlockSpec(memory_space=pl.ANY)
    return pl.pallas_call(
        body,
        name="attention_block",
        out_shape=jax.ShapeDtypeStruct((TB, WIDTH), BF),
        in_specs=[anywhere] * 7,
        out_specs=pl.BlockSpec(memory_space=pltpu.VMEM),
        scratch_shapes=scratch,
        compiler_params=pltpu.CompilerParams(collective_id=0, has_side_effects=True, vmem_limit_bytes=62 * 2**20),
        cost_estimate=pl.CostEstimate(flops=3 * 10**9, bytes_accessed=3 * 10**6, transcendentals=10**6),
    )(hidden_in, norm_gain.reshape(1, WIDTH), w_query, w_key, w_value, w_out, seg_lengths)


def solution(mesh):
    in_specs = (P("gy", "gx"), P("gx"), P("gx", "gy"), P("gx", None), P("gx", None), P("gy", "gx"), P())
    return jax.shard_map(shards, mesh=mesh, in_specs=in_specs, out_specs=P("gy", "gx"), check_vma=False)
```
